256 devices in a mesh: dp: 2 (over core), tm: 8 (over x_lo, y), height: 16 (over z, x_hi).
Axes of the slice: x: 4 (x_hi: 2, x_lo: 2; x = x_hi * 2 + x_lo), y: 4, z: 8, core: 2. Of those that a mesh axis runs over, the one named last changes fastest.
Arguments:
- inputs: bfloat16 [2, 32, 32, 192, 128], P('dp', 'tm', 'height'), may hold values from -6 to 6
- gain_in: float32 [192], replicated, may hold values from 0.5 to 1.5
- conv_in: bfloat16 [3, 3, 3, 96, 192], replicated, may hold values from -0.078125 to 0.078125
- gain_mid: float32 [96], replicated, may hold values from 0.5 to 1.5
- conv_mid: bfloat16 [3, 3, 3, 96, 96], replicated, may hold values from -0.125 to 0.125
- conv_skip: bfloat16 [96, 192], replicated, may hold values from -0.4375 to 0.4375
- scored_grads: bfloat16 [2, 16, 32, 96, 128], P('dp', 'tm', 'height'), may hold values from -6 to 6
- scored_frames: int32 [2, 16], P('dp'), may hold values from 0 to 31, as said below
Outputs:
- grad_inputs: bfloat16 [2, 32, 32, 192, 128], P('dp', 'tm', 'height')
- grad_conv_in: float32 [3, 3, 3, 96, 192], replicated
- grad_conv_mid: float32 [3, 3, 3, 96, 96], replicated
- grad_conv_skip: float32 [96, 192], replicated
The draws below stay inside these ranges and needn't reach their ends.
Inputs may be any that keep to these rules, and one draw needn't show every extreme that they name: `scored_frames`: each clip's 16 entries are distinct frame numbers and always include 0 and 31.
All inputs are finite; a program needn't handle non-finite values.
Results may differ from the reference program's by a relative error of at most 0.013.
Values may be sent and summed in bfloat16 or wider, within the bound.
A program may use at most 64 MiB of HBM per device.

```python
import math
import jax
import jax.numpy as jnp
from jax import lax

C_IN = 192
C_OUT = 96
W_COLS = 128
CLIPS = 2
FRAMES = 32
ROWS = 32
SCORED = 16


def draw_scored_frames(key, part):
    key = jax.random.fold_in(key, 7)
    keys = jax.random.split(key, CLIPS)

    def one_clip(clip_key):
        inner = jax.random.permutation(clip_key, FRAMES - 2).astype(jnp.int32) + 1
        ends = jnp.array([0, FRAMES - 1], dtype=jnp.int32)
        return jnp.concatenate([ends, inner[:SCORED - 2]])
    return jax.vmap(one_clip)(keys).astype(jnp.int32)


def steps_of(rng, dims, shards, least, largest):
    def one(axis_at, blocks):
        heights = jax.random.uniform(jax.random.fold_in(jax.random.fold_in(rng, 6), axis_at), (blocks,), jnp.float32, least / len(shards), largest / len(shards))
        return jnp.repeat(jnp.exp(heights), dims[axis_at] // blocks).reshape((-1,) + (1,) * (len(dims) - axis_at - 1))

    level = one(*shards[0])
    for cut in shards[1:]:
        level = level * one(*cut)
    return level


def noise(stream_key, dims, width, limit, cuts=(), kind=jnp.bfloat16):
    values = jax.random.normal(stream_key, dims, jnp.float32) * width
    if len(cuts) > 0:
        values = steps_of(stream_key, dims, cuts, -0.22, 0.18) * values
    return jnp.clip(values, min=-limit, max=limit).astype(kind)


def setup_inputs(seed: int = 0) -> dict:
    splits = jax.random.split(jax.random.key(seed), 9)
    return {
        "inputs": noise(splits[0], (CLIPS, FRAMES, ROWS, C_IN, W_COLS), 1.0, 6.0, ((0, 2), (1, 8), (2, 16))),
        "gain_in": jnp.clip(jax.random.uniform(splits[1], (C_IN,), jnp.float32, 0.5, 1.5), 0.5, 1.5),
        "conv_in": noise(splits[2], (3, 3, 3, C_OUT, C_IN), (27 * C_IN) ** -0.5, 0.078125),
        "gain_mid": jnp.clip(jax.random.uniform(splits[3], (C_OUT,), jnp.float32, 0.5, 1.5), 0.5, 1.5),
        "conv_mid": noise(splits[4], (3, 3, 3, C_OUT, C_OUT), (27 * C_OUT) ** -0.5, 0.125),
        "conv_skip": noise(splits[5], (C_OUT, C_IN), C_IN ** -0.5, 0.4375),
        "scored_grads": noise(splits[6], (CLIPS, SCORED, ROWS, C_OUT, W_COLS), 1.0, 6.0, ((0, 2), (1, 8), (2, 16))),
        "scored_frames": draw_scored_frames(jax.random.fold_in(splits[8], 71), 0),
    }


def act_norm(field, gain):
    mean_sq = lax.optimization_barrier(jnp.mean(field * field, axis=2, keepdims=True))
    return jax.nn.silu(field * lax.rsqrt(mean_sq + 1e-06) * gain[:, None])

def shifted_stack(padded, cols, offsets):
    return jnp.concatenate([padded[..., k:k + cols] for k in offsets], axis=2)

def taps_forward(padded, weight, frames, rows, cols):
    stack = shifted_stack(padded, cols, (0, 1, 2))
    out_ch = weight.shape[3]
    total = jnp.zeros((frames, rows, out_ch, cols), jnp.float32)
    for kt in range(3):
        for kh in range(3):
            matrix = weight[kt, kh].transpose(1, 0, 2).reshape(out_ch, -1).astype(jnp.float32)
            window = stack[kt:kt + frames, kh:kh + rows].astype(jnp.float32)
            total = total + jnp.einsum('om,fhmw->fhow', matrix, window)
    return total

def taps_input(padded, weight, frames, rows, cols):
    stack = shifted_stack(padded, cols, (2, 1, 0))
    in_ch = weight.shape[4]
    total = jnp.zeros((frames, rows, in_ch, cols), jnp.float32)
    for kt in range(3):
        for kh in range(3):
            matrix = weight[kt, kh].reshape(-1, in_ch).astype(jnp.float32)
            window = stack[2 - kt:2 - kt + frames, 2 - kh:2 - kh + rows].astype(jnp.float32)
            total = total + jnp.einsum('mc,fhmw->fhcw', matrix, window)
    return total

def taps_weight(grad, padded, frames, rows, cols):
    stack = shifted_stack(padded, cols, (0, 1, 2))
    out_ch = grad.shape[2]
    in_ch = padded.shape[2]
    grad_f = grad.astype(jnp.float32)
    pieces = []
    for kt in range(3):
        for kh in range(3):
            window = stack[kt:kt + frames, kh:kh + rows].astype(jnp.float32)
            block = jnp.einsum('fhow,fhmw->om', grad_f, window)
            pieces.append(block.reshape(out_ch, 3, in_ch).transpose(1, 0, 2))
    return jnp.stack(pieces).reshape(3, 3, 3, out_ch, in_ch)

def pad_prior(field):
    return jnp.pad(field, ((2, 0), (1, 1), (0, 0), (1, 1)))

def pad_after(field):
    return jnp.pad(field, ((0, 2), (1, 1), (0, 0), (1, 1)))

def reference(inputs, gain_in, conv_in, gain_mid, conv_mid, conv_skip, scored_grads, scored_frames):
    scale = 1.0 / math.sqrt(CLIPS * SCORED * ROWS * W_COLS)
    grads_x = []
    sum_in = jnp.zeros(conv_in.shape, jnp.float32)
    sum_mid = jnp.zeros(conv_mid.shape, jnp.float32)
    sum_skip = jnp.zeros(conv_skip.shape, jnp.float32)
    for clip in range(CLIPS):
        x_clip = inputs[clip]
        h1 = act_norm(x_clip.astype(jnp.float32), gain_in).astype(jnp.bfloat16)
        h1_pad = pad_prior(h1)
        a1 = taps_forward(h1_pad, conv_in, FRAMES, ROWS, W_COLS).astype(jnp.bfloat16)
        h2 = act_norm(a1.astype(jnp.float32), gain_mid).astype(jnp.bfloat16)
        chosen = (scored_frames[clip][None, :] == jnp.arange(FRAMES, dtype=jnp.int32)[:, None]).astype(jnp.float32)
        cot = jnp.einsum('fj,jhow->fhow', chosen, scored_grads[clip].astype(jnp.float32)).astype(jnp.bfloat16)
        sum_mid = sum_mid + scale * taps_weight(cot, pad_prior(h2), FRAMES, ROWS, W_COLS)
        sum_skip = sum_skip + scale * jnp.einsum('fhow,fhcw->oc', cot.astype(jnp.float32), x_clip.astype(jnp.float32))
        gh2 = taps_input(pad_after(cot), conv_mid, FRAMES, ROWS, W_COLS)
        _, pull_mid = jax.vjp(lambda v: act_norm(v, gain_mid), a1.astype(jnp.float32))
        ga1 = pull_mid(gh2)[0].astype(jnp.bfloat16)
        sum_in = sum_in + scale * taps_weight(ga1, h1_pad, FRAMES, ROWS, W_COLS)
        gh1 = taps_input(pad_after(ga1), conv_in, FRAMES, ROWS, W_COLS)
        _, pull_in = jax.vjp(lambda v: act_norm(v, gain_in), x_clip.astype(jnp.float32))
        skip_back = jnp.einsum('oc,fhow->fhcw', conv_skip.astype(jnp.float32), cot.astype(jnp.float32))
        grads_x.append((pull_in(gh1)[0] + skip_back).astype(jnp.bfloat16))
    return (jnp.stack(grads_x), sum_in, sum_mid, sum_skip)
```

```python
import math

import jax
import jax.numpy as jnp
from jax import lax
from jax.experimental import pallas as pl
from jax.experimental.pallas import tpu as pltpu
from jax.sharding import PartitionSpec as P

MESH = pl.DeviceIdType.MESH
F32 = jnp.float32
BF16 = jnp.bfloat16
FR, RW, CI, CO, W = 4, 2, 192, 96, 128
TM, HT = 8, 16
SC = 2
EPS = 1e-06
TAPS = [(kt, kh) for kt in range(3) for kh in range(3)]
PAIRS = [(0, 1), (2, 3), (4, 5), (6, 7)]
ROWS_IN, ROWS_MID = 4096, 2048


def sigmoid(u):
    return 1.0 / (1.0 + jnp.exp(-u))


def norm_parts(v, g):
    s = lax.rsqrt(jnp.mean(v * v, axis=0, keepdims=True) + EPS)
    n = v * s
    u = n * g
    return s, n, u, sigmoid(u)


def norm_fwd(v, g):
    _, _, u, sg = norm_parts(v, g)
    return u * sg


def norm_pull(v, g, ct):
    s, n, u, sg = norm_parts(v, g)
    dn = ct * (sg * (1.0 + u * (1.0 - sg))) * g
    return s * (dn - n * jnp.mean(dn * n, axis=0, keepdims=True))


def ahead(v):
    lane = lax.broadcasted_iota(jnp.int32, v.shape, 1)
    return jnp.where(lane == W - 1, 0.0, pltpu.roll(v, W - 1, 1))


def behind(v):
    lane = lax.broadcasted_iota(jnp.int32, v.shape, 1)
    return jnp.where(lane == 0, 0.0, pltpu.roll(v, 1, 1))


def column(row, n):
    r = lax.broadcasted_iota(jnp.int32, (n, n), 0)
    c = lax.broadcasted_iota(jnp.int32, (n, n), 1)
    return jnp.sum(jnp.where(r == c, jnp.broadcast_to(row, (n, n)), 0.0), axis=1, keepdims=True)


def dot(a, b):
    return jnp.dot(a, b, preferred_element_type=F32)


def dot_nt(a, b):
    return lax.dot_general(a, b, (((1,), (1,)), ((), ())), preferred_element_type=F32)


def pair(ref, f, r):
    return jnp.concatenate([ref[f, r], ref[f, r + 1]], axis=1)


class Sems:
    def __init__(self, send, recv):
        self.send, self.recv, self.n = send, recv, 0

    def take(self, count):
        at = self.n
        self.n += count
        return list(range(at, at + count))


N_SEMS = 120
N_LOCAL = 8


def when(cond, fn):
    if cond is None:
        fn()
    else:
        pl.when(cond)(fn)


def kernel(scale, sf, x_hbm, gain_in, win_hbm, gain_mid, wmid_hbm, wskip, sg_hbm,
           out_x, out_in, out_mid, out_skip,
           XE, H1, SG, CE, CS, GE, GS, A1, H2, WIN, WMID, WTI, WTM,
           g_in, g_mid, rc_in, rc_mid, s_in, s_mid,
           a1_in, b1_in, a1_mid, b1_mid, p_in, p_mid, a2_in, b2_in, a2_mid, b2_mid,
           c_in, c_mid, z_in, z_mid, fin_in, fin_mid,
           send, recv, local):
    c = lax.axis_index("dp")
    t = lax.axis_index("tm")
    h = lax.axis_index("height")
    y, x_lo = t % 4, t // 4
    z, x_hi = h // 2, h % 2
    xx = x_hi * 2 + x_lo
    sems = Sems(send, recv)
    sent = []

    def dev(tt=None, hh=None, cc=None):
        d = {}
        d["dp"] = c if cc is None else cc
        d["tm"] = t if tt is None else tt
        d["height"] = h if hh is None else hh
        return d

    def x_peer(v):
        return dev(tt=y + 4 * (v % 2), hh=z * 2 + v // 2)

    def y_peer(v):
        return dev(tt=x_lo * 4 + v)

    def z_peer(v):
        return dev(hh=v * 2 + x_hi)

    class Copy:
        def __init__(self, src, dst, to, s_if=None, r_if=None):
            i = sems.take(1)[0]
            self.d = pltpu.make_async_remote_copy(
                src_ref=src, dst_ref=dst, send_sem=send.at[i], recv_sem=recv.at[i],
                device_id=to, device_id_type=MESH)
            self.s_if, self.r_if = s_if, r_if

        def start(self):
            when(self.s_if, lambda: self.d.start())
            sent.append(self)

        def got(self):
            when(self.r_if, lambda: self.d.wait_recv())

        def left(self):
            when(self.s_if, lambda: self.d.wait_send())

    loc = [
        pltpu.make_async_copy(x_hbm.at[0], XE.at[pl.ds(2, FR), pl.ds(1, RW)], local.at[0]),
        pltpu.make_async_copy(sg_hbm.at[0], SG.at[pl.ds(SC * t, SC)], local.at[1]),
        pltpu.make_async_copy(win_hbm, WIN, local.at[2]),
        pltpu.make_async_copy(wmid_hbm, WMID, local.at[3]),
    ]
    for item in loc:
        item.start()

    barrier = pltpu.get_barrier_semaphore()
    friends = [dev(tt=(t + k) % TM) for k in range(1, TM)]
    friends += [dev(hh=(h + k) % HT) for k in (1, 15, 2, 4, 6, 8, 10, 12, 14)]
    friends += [dev(tt=(t + a) % TM, hh=(h + b) % HT) for a in (1, 7) for b in (1, 15)]
    friends += [x_peer(3 - xx), dev(cc=1 - c)]
    for to in friends:
        pl.semaphore_signal(barrier, inc=1, device_id=to, device_id_type=MESH)

    first_t, last_t, first_h, last_h = t == 0, t == TM - 1, h == 0, h == HT - 1

    def zero(ref, f0, nf, r0, nr, ch):
        def body():
            for f in range(f0, f0 + nf):
                for r in range(r0, r0 + nr):
                    ref[f, r] = jnp.zeros((ch, W), BF16)
        return body

    pl.when(first_t)(zero(XE, 0, 2, 0, 4, CI))
    pl.when(jnp.logical_and(first_h, t > 0))(zero(XE, 0, 2, 0, 1, CI))
    pl.when(jnp.logical_and(last_h, t > 0))(zero(XE, 0, 2, 3, 1, CI))
    pl.when(first_h)(zero(XE, 2, 4, 0, 1, CI))
    pl.when(last_h)(zero(XE, 2, 4, 3, 1, CI))
    pl.when(first_h)(zero(CE, 0, 6, 0, 1, CO))
    pl.when(last_h)(zero(CE, 0, 6, 3, 1, CO))
    pl.when(last_t)(zero(GE, 4, 2, 0, 4, CO))
    pl.when(jnp.logical_and(first_h, t < TM - 1))(zero(GE, 4, 2, 0, 1, CO))
    pl.when(jnp.logical_and(last_h, t < TM - 1))(zero(GE, 4, 2, 3, 1, CO))
    pl.when(first_h)(zero(GE, 0, 4, 0, 1, CO))
    pl.when(last_h)(zero(GE, 0, 4, 3, 1, CO))

    pl.semaphore_wait(barrier, len(friends))

    both = jnp.logical_and
    has_n, has_p = h < HT - 1, h > 0
    t_n, t_p = t < TM - 1, t > 0

    gather = [
        Copy(sg_hbm.at[0], SG.at[pl.ds(SC * t, SC)], dev(tt=(t + k) % TM)) for k in (1, 7, 2, 6, 3, 5, 4)
    ]
    for item in gather:
        item.start()

    src = x_hbm.at[0]
    x_halo = [
        Copy(src.at[:, 1], XE.at[pl.ds(2, 4), 0], dev(hh=h + 1), has_n, has_p),
        Copy(src.at[:, 0], XE.at[pl.ds(2, 4), 3], dev(hh=h - 1), has_p, has_n),
        Copy(src.at[pl.ds(2, 2)], XE.at[pl.ds(0, 2), pl.ds(1, 2)], dev(tt=t + 1), t_n, t_p),
        Copy(src.at[pl.ds(2, 2), 1], XE.at[pl.ds(0, 2), 0], dev(tt=t + 1, hh=h + 1),
             both(t_n, has_n), both(t_p, has_p)),
        Copy(src.at[pl.ds(2, 2), 0], XE.at[pl.ds(0, 2), 3], dev(tt=t + 1, hh=h - 1),
             both(t_n, has_p), both(t_p, has_n)),
    ]
    for item in x_halo:
        item.start()

    g1 = column(gain_in[...], CI)
    g2 = column(gain_mid[...], CO)

    def h1_at(f, r):
        H1[f, r] = norm_fwd(XE[f, r].astype(F32), g1).astype(BF16)

    loc[2].wait()
    loc[3].wait()

    def turn(i, _):
        kt, kh, kw = i // 9, (i // 3) % 3, i % 3
        WTI[i] = WIN[kt, kh, kw].astype(F32).T.astype(BF16)
        WTM[i] = WMID[kt, kh, kw].astype(F32).T.astype(BF16)
        return 0

    lax.fori_loop(0, 27, turn, 0)
    loc[0].wait()

    def h1_own(i, _):
        h1_at(2 + i // 2, 1 + i % 2)
        return 0

    lax.fori_loop(0, 8, h1_own, 0)

    loc[1].wait()
    for item in gather:
        item.got()
    for f in range(6):
        frame = t * FR + f
        at = jnp.int32(0)
        found = jnp.int32(0)
        for j in range(SC * TM):
            hit = (sf[0, j] == frame).astype(jnp.int32)
            at = jnp.maximum(at, j * hit)
            found = jnp.maximum(found, hit)
        factor = found.astype(F32)
        for r in range(RW):
            CE[f, 1 + r] = (SG[at, r].astype(F32) * factor).astype(BF16)
    cot_halo = [
        Copy(CE.at[:, 2], CE.at[:, 0], dev(hh=h + 1), has_n, has_p),
        Copy(CE.at[:, 1], CE.at[:, 3], dev(hh=h - 1), has_p, has_n),
    ]
    for item in cot_halo:
        item.start()

    skip_a = jnp.zeros((CO, W), F32)
    skip_b = jnp.zeros((CO, W), F32)
    for f in range(FR):
        cot = pair(CE, f, 1)
        xs = pair(XE, 2 + f, 1)
        skip_a = skip_a + dot_nt(cot, xs[:W])
        skip_b = skip_b + dot_nt(cot, jnp.concatenate([jnp.zeros((64, 2 * W), BF16), xs[W:]], axis=0))
    g_mid[pl.ds(2016, 32)] = skip_a[:32].astype(BF16)
    g_in[pl.ds(4032, 64)] = skip_a[32:].astype(BF16)

    for item in x_halo:
        item.got()

    def h1_rows(f, _):
        h1_at(f, 0)
        h1_at(f, 3)
        return 0

    def h1_prior(f, _):
        h1_at(f, 1)
        h1_at(f, 2)
        return 0

    lax.fori_loop(0, 6, h1_rows, 0)
    lax.fori_loop(0, 2, h1_prior, 0)

    def forward(f, _):
        acc = jnp.zeros((3 * CO, 2 * W), F32)
        for kt, kh in TAPS:
            acc = acc + dot(WIN[kt, kh].reshape(3 * CO, CI), pair(H1, f + kt, kh))
        for r in range(RW):
            part = acc[:, r * W:(r + 1) * W]
            a1 = part[CO:2 * CO] + behind(part[:CO]) + ahead(part[2 * CO:])
            a1 = a1.astype(BF16)
            A1[f, r] = a1
            H2[f, r] = norm_fwd(a1.astype(F32), g2).astype(BF16)
        return 0

    lax.fori_loop(0, FR, forward, 0)

    for item in cot_halo:
        item.got()

    def back_mid(f, _):
        acc = jnp.zeros((3 * CO, 2 * W), F32)
        for n, (kt, kh) in enumerate(TAPS):
            acc = acc + dot(WTM[pl.ds(3 * n, 3)].reshape(3 * CO, CO), pair(CE, f + 2 - kt, 2 - kh))
        for r in range(RW):
            part = acc[:, r * W:(r + 1) * W]
            gh2 = part[CO:2 * CO] + ahead(part[:CO]) + behind(part[2 * CO:])
            ga1 = norm_pull(A1[f, r].astype(F32), g2, gh2).astype(BF16)
            GE[f, 1 + r] = ga1
            wide = ga1.astype(F32)
            lanes = pl.ds(r * W, W)
            GS[f, pl.ds(0, CO), lanes] = ahead(wide).astype(BF16)
            GS[f, pl.ds(CO, CO), lanes] = ga1
            GS[f, pl.ds(2 * CO, CO), lanes] = behind(wide).astype(BF16)
        return 0

    lax.fori_loop(0, FR, back_mid, 0)
    ga_halo = [
        Copy(GE.at[pl.ds(0, 4), 2], GE.at[pl.ds(0, 4), 0], dev(hh=h + 1), has_n, has_p),
        Copy(GE.at[pl.ds(0, 4), 1], GE.at[pl.ds(0, 4), 3], dev(hh=h - 1), has_p, has_n),
        Copy(GE.at[pl.ds(0, 2), pl.ds(1, 2)], GE.at[pl.ds(4, 2), pl.ds(1, 2)], dev(tt=t - 1), t_p, t_n),
        Copy(GE.at[pl.ds(0, 2), 2], GE.at[pl.ds(4, 2), 0], dev(tt=t - 1, hh=h + 1),
             both(t_p, has_n), both(t_n, has_p)),
        Copy(GE.at[pl.ds(0, 2), 1], GE.at[pl.ds(4, 2), 3], dev(tt=t - 1, hh=h - 1),
             both(t_p, has_p), both(t_n, has_n)),
    ]
    for item in ga_halo:
        item.start()

    for n, taps in enumerate(PAIRS):
        acc = jnp.zeros((3 * CO, 3 * W), F32)
        for f in range(FR):
            one = [pair(H1, f + TAPS[i][0], TAPS[i][1]) for i in taps]
            rhs = jnp.concatenate([one[0][:W], one[1][:W], one[0][W:], one[1][W:]], axis=0)
            acc = acc + dot_nt(GS[f], rhs)
        for j in range(3):
            g_in[pl.ds(864 * n + 288 * j, 288)] = acc[:, j * W:(j + 1) * W].astype(BF16)
    acc = jnp.zeros((3 * CO, 2 * W), F32)
    for f in range(FR):
        one = pair(H1, f + 2, 2)
        rhs = jnp.concatenate([one, jnp.zeros((64, 2 * W), BF16)], axis=0)
        acc = acc + dot_nt(GS[f], rhs)
    for j in range(2):
        g_in[pl.ds(3456 + 288 * j, 288)] = acc[:, j * W:(j + 1) * W].astype(BF16)

    def reduce(g, rc, s, a1, b1, p, a2, b2, cc, zz, fin, rows):
        half = rows // 2
        ha = half // 2
        q = ha // 4
        e = q // 4
        owners = 2 * e // 16
        mine = pl.multiple_of(c * half, half)
        other = pl.multiple_of((1 - c) * half, half)

        def at(off, n):
            return pl.ds(pl.multiple_of(off, 16), n)

        def total(terms):
            out = terms[0].astype(F32)
            for term in terms[1:]:
                out = out + term.astype(F32)
            return out.astype(BF16)

        step = 128

        core = Copy(g.at[pl.ds(other, half)], rc, dev(cc=1 - c))
        core.start()
        yield
        core.got()

        def add_core(i, _):
            o = pl.multiple_of(i * step, step)
            s[pl.ds(o, step)] = total([g[pl.ds(pl.multiple_of(mine + o, step), step)], rc[pl.ds(o, step)]])
            return 0

        lax.fori_loop(0, half // step, add_core, 0)
        one = []
        for k in (1, 3, 2):
            xp, yp = (xx + k) % 4, (y + k) % 4
            one.append(Copy(s.at[at(xp * q, q)], a1.at[k - 1], x_peer(xp)))
            one.append(Copy(s.at[at(ha + yp * q, q)], b1.at[k - 1], y_peer(yp)))
        for item in one:
            item.start()
        yield
        for item in one:
            item.got()
        p[pl.ds(0, q)] = total([s[at(xx * q, q)], a1[0], a1[1], a1[2]])
        p[pl.ds(q, q)] = total([s[at(ha + y * q, q)], b1[0], b1[1], b1[2]])
        two = []
        for k in (1, 3, 2):
            xp, yp = (xx + k) % 4, (y + k) % 4
            two.append(Copy(p.at[at(yp * e, e)], a2.at[k - 1], y_peer(yp)))
            two.append(Copy(p.at[at(q + xp * e, e)], b2.at[k - 1], x_peer(xp)))
        for item in two:
            item.start()
        yield
        for item in two:
            item.got()
        cc[pl.ds(0, e)] = total([p[at(y * e, e)], a2[0], a2[1], a2[2]])
        cc[pl.ds(e, e)] = total([p[at(q + xx * e, e)], b2[0], b2[1], b2[2]])
        ks = (1, 7, 2, 6, 3, 5, 4)
        own = None if owners == 8 else z < owners
        three = []
        for k in ks:
            zp = (z + k) % 8
            three.append(Copy(cc.at[at(zp % owners * 16, 16)], zz.at[k - 1], z_peer(zp),
                              None if owners == 8 else zp < owners, own))
        for item in three:
            item.start()
        yield
        for item in three:
            item.got()
        chain_b = (z >= owners // 2).astype(jnp.int32)
        zt = z % (owners // 2)
        base_a = mine + xx * q + y * e
        base_b = mine + ha + y * q + xx * e
        place = base_a + chain_b * (base_b - base_a) + zt * 16

        def finish():
            fin[at(place, 16)] = total([cc[at(z % owners * 16, 16)]] + [zz[k] for k in range(7)])

        when(own, finish)
        four = []
        for k in ks:
            zp, zm = (z + k) % 8, (z + 8 - k) % 8
            four.append(Copy(fin.at[at(place, 16)], fin.at[at(place, 16)], z_peer(zp),
                             own, None if owners == 8 else zm < owners))
        for item in four:
            item.start()
        yield
        for item in four:
            item.got()
        five = []
        for k in (1, 3, 2):
            xp, yp = (xx + k) % 4, (y + k) % 4
            five.append(Copy(fin.at[at(base_a, e)], fin.at[at(base_a, e)], y_peer(yp)))
            five.append(Copy(fin.at[at(base_b, e)], fin.at[at(base_b, e)], x_peer(xp)))
        for item in five:
            item.start()
        yield
        for item in five:
            item.got()
        six = []
        for k in (1, 3, 2):
            xp, yp = (xx + k) % 4, (y + k) % 4
            six.append(Copy(fin.at[at(mine + xx * q, q)], fin.at[at(mine + xx * q, q)], x_peer(xp)))
            six.append(Copy(fin.at[at(mine + ha + y * q, q)], fin.at[at(mine + ha + y * q, q)], y_peer(yp)))
        for item in six:
            item.start()
        yield
        for item in six:
            item.got()
        last = Copy(fin.at[pl.ds(mine, half)], fin.at[pl.ds(mine, half)], dev(cc=1 - c))
        last.start()
        yield
        last.got()
        yield

    big = reduce(g_in, rc_in, s_in, a1_in, b1_in, p_in, a2_in, b2_in, c_in, z_in, fin_in, ROWS_IN)
    small = reduce(g_mid, rc_mid, s_mid, a1_mid, b1_mid, p_mid, a2_mid, b2_mid, c_mid, z_mid, fin_mid, ROWS_MID)
    next(big)

    def cot_shift(f, _):
        for r in range(4):
            wide = CE[f, r].astype(F32)
            lanes = pl.ds(r * W, W)
            CS[f, pl.ds(0, CO), lanes] = ahead(wide).astype(BF16)
            CS[f, pl.ds(CO, CO), lanes] = CE[f, r]
            CS[f, pl.ds(2 * CO, CO), lanes] = behind(wide).astype(BF16)
        return 0

    lax.fori_loop(0, 6, cot_shift, 0)

    def cot_window(f, tap):
        kt, kh = TAPS[tap]
        return CS[f + 2 - kt, :, pl.ds((2 - kh) * W, 2 * W)]

    for n in range(2):
        acc = jnp.zeros((CO, 9 * W), F32)
        for f in range(FR):
            rhs = jnp.concatenate([cot_window(f, 4 * n + i) for i in range(4)], axis=0)
            acc = acc + dot_nt(pair(H2, f, 0), rhs)
        for j in range(9):
            g_mid[pl.ds(864 * n + CO * j, CO)] = acc[:, j * W:(j + 1) * W].astype(BF16)
    acc = jnp.zeros((CO, 3 * W), F32)
    for f in range(FR):
        rhs = jnp.concatenate([cot_window(f, 8), jnp.zeros((CO, 2 * W), BF16)], axis=0)
        acc = acc + dot_nt(pair(H2, f, 0), rhs)
    g_mid[pl.ds(1728, CO)] = acc[:, :W].astype(BF16)
    g_mid[pl.ds(1824, CO)] = acc[:, W:2 * W].astype(BF16)
    g_mid[pl.ds(1920, CO)] = (acc[:, 2 * W:] + skip_b).astype(BF16)

    next(small)
    next(big)
    next(small)

    def back_in(f):
        acc = jnp.zeros((3 * CI, 2 * W), F32)
        for n, (kt, kh) in enumerate(TAPS):
            acc = acc + dot(WTI[pl.ds(3 * n, 3)].reshape(3 * CI, CO), pair(GE, f + 2 - kt, 2 - kh))
        skip = lax.dot_general(wskip[...], pair(CE, f, 1), (((0,), (0,)), ((), ())),
                               preferred_element_type=F32)
        for r in range(RW):
            part = acc[:, r * W:(r + 1) * W]
            gh1 = part[CI:2 * CI] + ahead(part[:CI]) + behind(part[2 * CI:])
            grad = norm_pull(XE[2 + f, 1 + r].astype(F32), g1, gh1) + skip[:, r * W:(r + 1) * W]
            out_x[0, f, r] = grad.astype(BF16)

    for item in ga_halo:
        item.got()
    for f in range(FR):
        back_in(f)
        next(big)
        next(small)
    for _ in range(2):
        next(big)
        next(small)
    next(big)

    for n, taps in enumerate(PAIRS):
        for kw in range(3):
            low = fin_in[pl.ds(864 * n + 576 + CO * kw, CO)].astype(F32) * scale
            for j, i in enumerate(taps):
                kt, kh = TAPS[i]
                high = fin_in[pl.ds(864 * n + 288 * j + CO * kw, CO)].astype(F32) * scale
                out_in[kt, kh, kw, :, pl.ds(0, W)] = high
                rest = low if j == 0 else pltpu.roll(low, 64, 1)
                out_in[kt, kh, kw, :, pl.ds(W, 64)] = rest[:, :64]
    for kw in range(3):
        out_in[2, 2, kw, :, pl.ds(0, W)] = fin_in[pl.ds(3456 + CO * kw, CO)].astype(F32) * scale
        out_in[2, 2, kw, :, pl.ds(W, 64)] = (fin_in[pl.ds(3744 + CO * kw, CO)].astype(F32) * scale)[:, :64]
    out_skip[pl.ds(32, 64), pl.ds(0, W)] = fin_in[pl.ds(4032, 64)].astype(F32) * scale
    next(small)
    for j in range(20):
        out_mid[pl.ds(W * j, W)] = (fin_mid[pl.ds(CO * j, CO)].astype(F32) * scale).T
    tail = fin_mid[pl.ds(1920, CO)].astype(F32) * scale
    out_mid[pl.ds(2560, 32)] = tail.T[:32]
    out_skip[:, pl.ds(W, 64)] = pltpu.roll(tail, 64, 1)[:, :64]
    out_skip[pl.ds(0, 32), pl.ds(0, W)] = fin_mid[pl.ds(2016, 32)].astype(F32) * scale

    for item in sent:
        item.left()


def reduce_scratch(rows):
    half = rows // 2
    q, e = half // 8, half // 32
    return {
        "g": (rows, W), "rc": (half, W), "s": (half, W), "a1": (3, q, W), "b1": (3, q, W), "p": (2 * q, W),
        "a2": (3, e, W), "b2": (3, e, W), "c": (2 * e, W), "z": (7, 16, W), "fin": (rows, W),
    }


def shards(inputs, gain_in, conv_in, gain_mid, conv_mid, conv_skip, scored_grads, scored_frames):
    count = scored_frames.shape[1] * inputs.shape[0] * lax.axis_size("dp")
    scale = 1.0 / math.sqrt(count * RW * HT * W)
    vmem = pl.BlockSpec(memory_space=pltpu.VMEM)
    anyw = pl.BlockSpec(memory_space=pl.ANY)
    smem = pl.BlockSpec(memory_space=pltpu.SMEM)
    big, small = reduce_scratch(ROWS_IN), reduce_scratch(ROWS_MID)

    def buf(shape, dtype=BF16):
        return pltpu.VMEM(shape, dtype)

    scratch = [
        buf((6, 4, CI, W)), buf((6, 4, CI, W)), buf((SC * TM, RW, CO, W)), buf((6, 4, CO, W)),
        buf((6, 3 * CO, 4 * W)), buf((6, 4, CO, W)), buf((FR, 3 * CO, RW * W)),
        buf((FR, RW, CO, W)), buf((FR, RW, CO, W)),
        buf((3, 3, 3, CO, CI)), buf((3, 3, 3, CO, CO)), buf((27, CI, CO)), buf((27, CO, CO)),
    ]
    for name in ("g", "rc", "s"):
        scratch += [buf(big[name]), buf(small[name])]
    scratch += [buf(big["a1"]), buf(big["b1"]), buf(small["a1"]), buf(small["b1"])]
    scratch += [buf(big["p"]), buf(small["p"])]
    scratch += [buf(big["a2"]), buf(big["b2"]), buf(small["a2"]), buf(small["b2"])]
    for name in ("c", "z", "fin"):
        scratch += [buf(big[name]), buf(small[name])]
    scratch += [
        pltpu.SemaphoreType.DMA((N_SEMS,)), pltpu.SemaphoreType.DMA((N_SEMS,)),
        pltpu.SemaphoreType.DMA((N_LOCAL,)),
    ]

    def body(*refs):
        kernel(scale, *refs)

    grad_inputs, grad_in, grad_mid, grad_skip = pl.pallas_call(
        body,
        out_shape=(
            jax.ShapeDtypeStruct(inputs.shape, BF16),
            jax.ShapeDtypeStruct(conv_in.shape, F32),
            jax.ShapeDtypeStruct((27 * CO, CO), F32),
            jax.ShapeDtypeStruct(conv_skip.shape, F32),
        ),
        in_specs=[smem, anyw, vmem, anyw, vmem, anyw, vmem, anyw],
        out_specs=(vmem, vmem, vmem, vmem),
        scratch_shapes=scratch,
        compiler_params=pltpu.CompilerParams(
            collective_id=0, has_side_effects=True, vmem_limit_bytes=48 * 1024 * 1024
        ),
        name="block_backward",
    )(scored_frames, inputs, gain_in[None, :], conv_in, gain_mid[None, :], conv_mid, conv_skip, scored_grads)
    return grad_inputs, grad_in, grad_mid.reshape(conv_mid.shape), grad_skip


def solution(mesh):
    in_specs = (
        P("dp", "tm", "height", None, None),
        P(),
        P(),
        P(),
        P(),
        P(),
        P("dp", "tm", "height", None, None),
        P("dp", None),
    )
    out_specs = (P("dp", "tm", "height", None, None), P(), P(), P())
    return jax.shard_map(shards, mesh=mesh, in_specs=in_specs, out_specs=out_specs, check_vma=False)
```

```python
import math

import jax
import jax.numpy as jnp
from jax import lax
from jax.experimental import pallas as pl
from jax.experimental.pallas import tpu as pltpu
from jax.sharding import PartitionSpec as P

MESH = pl.DeviceIdType.MESH
F32 = jnp.float32
BF16 = jnp.bfloat16
FR, RW, CI, CO, W = 4, 2, 192, 96, 128
TM, HT = 8, 16
SC = 2
EPS = 1e-06
TAPS = [(kt, kh) for kt in range(3) for kh in range(3)]
PAIRS = [(0, 1), (2, 3), (4, 5), (6, 7)]
ROWS_IN, ROWS_MID = 4096, 2048


def sigmoid(u):
    return 1.0 / (1.0 + jnp.exp(-u))


def norm_parts(v, g):
    s = lax.rsqrt(jnp.mean(v * v, axis=0, keepdims=True) + EPS)
    n = v * s
    u = n * g
    return s, n, u, sigmoid(u)


def norm_fwd(v, g):
    _, _, u, sg = norm_parts(v, g)
    return u * sg


def norm_pull(v, g, ct):
    s, n, u, sg = norm_parts(v, g)
    dn = ct * (sg * (1.0 + u * (1.0 - sg))) * g
    return s * (dn - n * jnp.mean(dn * n, axis=0, keepdims=True))


def ahead(v):
    lane = lax.broadcasted_iota(jnp.int32, v.shape, 1)
    return jnp.where(lane == W - 1, 0.0, pltpu.roll(v, W - 1, 1))


def behind(v):
    lane = lax.broadcasted_iota(jnp.int32, v.shape, 1)
    return jnp.where(lane == 0, 0.0, pltpu.roll(v, 1, 1))


def column(row, n):
    r = lax.broadcasted_iota(jnp.int32, (n, n), 0)
    c = lax.broadcasted_iota(jnp.int32, (n, n), 1)
    return jnp.sum(jnp.where(r == c, jnp.broadcast_to(row, (n, n)), 0.0), axis=1, keepdims=True)


def dot(a, b):
    return jnp.dot(a, b, preferred_element_type=F32)


def dot_nt(a, b):
    return lax.dot_general(a, b, (((1,), (1,)), ((), ())), preferred_element_type=F32)


def pair(ref, f, r):
    return jnp.concatenate([ref[f, r], ref[f, r + 1]], axis=1)


class Sems:
    def __init__(self, send, recv):
        self.send, self.recv, self.n = send, recv, 0

    def take(self, count):
        at = self.n
        self.n += count
        return list(range(at, at + count))


N_SEMS = 192
N_LOCAL = 24


def when(cond, fn):
    if cond is None:
        fn()
    else:
        pl.when(cond)(fn)


def kernel(scale, sf, x_hbm, gain_in, win_hbm, gain_mid, wmid_hbm, wskip, sg_hbm,
           out_x, out_in, out_mid,
           OX,           XE, H1, SG, CE, CS, GE, GS, A1, H2, WIN, WMID, WTI, WTM,
           g_in, g_mid, rc_in, rc_mid, s_in, s_mid,
           a1_in, b1_in, a1_mid, b1_mid, p_in, p_mid, a2_in, b2_in, a2_mid, b2_mid,
           c_in, c_mid, z_in, z_mid, fin_in, fin_mid,
           send, recv, local):
    c = lax.axis_index("dp")
    t = lax.axis_index("tm")
    h = lax.axis_index("height")
    y, x_lo = t % 4, t // 4
    z, x_hi = h // 2, h % 2
    xx = x_hi * 2 + x_lo
    sems = Sems(send, recv)
    sent = []

    def dev(tt=None, hh=None, cc=None):
        d = {}
        d["dp"] = c if cc is None else cc
        d["tm"] = t if tt is None else tt
        d["height"] = h if hh is None else hh
        return d

    def x_peer(v):
        return dev(tt=y + 4 * (v % 2), hh=z * 2 + v // 2)

    def y_peer(v):
        return dev(tt=x_lo * 4 + v)

    def z_peer(v):
        return dev(hh=v * 2 + x_hi)

    kept = []

    def keep(src, dst):
        copy = pltpu.make_async_copy(src, dst, local.at[4 + len(kept)])
        copy.start()
        kept.append(copy)

    class Copy:
        def __init__(self, src, dst, to, s_if=None, r_if=None):
            i = sems.take(1)[0]
            self.d = pltpu.make_async_remote_copy(
                src_ref=src, dst_ref=dst, send_sem=send.at[i], recv_sem=recv.at[i],
                device_id=to, device_id_type=MESH)
            self.s_if, self.r_if = s_if, r_if

        def start(self):
            when(self.s_if, lambda: self.d.start())
            sent.append(self)

        def got(self):
            when(self.r_if, lambda: self.d.wait_recv())

        def left(self):
            when(self.s_if, lambda: self.d.wait_send())

    loc = [
        pltpu.make_async_copy(x_hbm.at[0], XE.at[pl.ds(2, FR), pl.ds(1, RW)], local.at[0]),
        pltpu.make_async_copy(sg_hbm.at[0], SG.at[pl.ds(SC * t, SC)], local.at[1]),
        pltpu.make_async_copy(win_hbm, WIN, local.at[2]),
        pltpu.make_async_copy(wmid_hbm, WMID, local.at[3]),
    ]
    for item in loc:
        item.start()

    barrier = pltpu.get_barrier_semaphore()
    friends = [y_peer((y + k) % 4) for k in (1, 2, 3)]
    friends += [dev(tt=(t + k) % TM) for k in (1, 7, 4)]
    friends += [dev(hh=(h + k) % HT) for k in (1, 15, 2, 4, 6, 8, 10, 12, 14)]
    friends += [dev(tt=(t + a) % TM, hh=(h + b) % HT) for a in (1, 7) for b in (1, 15)]
    friends += [x_peer(3 - xx), dev(cc=1 - c)]
    for to in friends:
        pl.semaphore_signal(barrier, inc=1, device_id=to, device_id_type=MESH)

    first_t, last_t, first_h, last_h = t == 0, t == TM - 1, h == 0, h == HT - 1

    def zero(ref, f0, nf, r0, nr, ch):
        def body():
            for f in range(f0, f0 + nf):
                for r in range(r0, r0 + nr):
                    ref[f, r] = jnp.zeros((ch, W), BF16)
        return body

    pl.when(first_t)(zero(XE, 0, 2, 0, 4, CI))
    pl.when(jnp.logical_and(first_h, t > 0))(zero(XE, 0, 2, 0, 1, CI))
    pl.when(jnp.logical_and(last_h, t > 0))(zero(XE, 0, 2, 3, 1, CI))
    pl.when(first_h)(zero(XE, 2, 4, 0, 1, CI))
    pl.when(last_h)(zero(XE, 2, 4, 3, 1, CI))
    pl.when(first_h)(zero(CE, 0, 6, 0, 1, CO))
    pl.when(last_h)(zero(CE, 0, 6, 3, 1, CO))
    pl.when(last_t)(zero(GE, 4, 2, 0, 4, CO))
    pl.when(jnp.logical_and(first_h, t < TM - 1))(zero(GE, 4, 2, 0, 1, CO))
    pl.when(jnp.logical_and(last_h, t < TM - 1))(zero(GE, 4, 2, 3, 1, CO))
    pl.when(first_h)(zero(GE, 0, 4, 0, 1, CO))
    pl.when(last_h)(zero(GE, 0, 4, 3, 1, CO))

    pl.semaphore_wait(barrier, len(friends))

    both = jnp.logical_and
    has_n, has_p = h < HT - 1, h > 0
    t_n, t_p = t < TM - 1, t > 0

    other_t = (t + TM // 2) % TM
    across = [Copy(sg_hbm.at[0, j], SG.at[SC * t + j], dev(tt=other_t)) for j in range(SC)]
    along = [Copy(sg_hbm.at[0], SG.at[pl.ds(SC * t, SC)], y_peer((y + k) % 4)) for k in (1, 3, 2)]
    for item in across + along:
        item.start()

    src = x_hbm.at[0]
    x_halo = [
        Copy(src.at[:, 1], XE.at[pl.ds(2, 4), 0], dev(hh=h + 1), has_n, has_p),
        Copy(src.at[:, 0], XE.at[pl.ds(2, 4), 3], dev(hh=h - 1), has_p, has_n),
        Copy(src.at[pl.ds(2, 2)], XE.at[pl.ds(0, 2), pl.ds(1, 2)], dev(tt=t + 1), t_n, t_p),
        Copy(src.at[pl.ds(2, 2), 1], XE.at[pl.ds(0, 2), 0], dev(tt=t + 1, hh=h + 1),
             both(t_n, has_n), both(t_p, has_p)),
        Copy(src.at[pl.ds(2, 2), 0], XE.at[pl.ds(0, 2), 3], dev(tt=t + 1, hh=h - 1),
             both(t_n, has_p), both(t_p, has_n)),
    ]
    for item in x_halo[:2]:
        item.start()

    for j in range(SC):
        across[j].got()
        at_j = SC * other_t + j
        onward = [Copy(SG.at[at_j], SG.at[at_j], y_peer((y + k) % 4)) for k in (1, 3, 2)]
        for item in onward:
            item.start()
        along += onward
    for item in x_halo[2:]:
        item.start()

    g1 = column(gain_in[...], CI)
    g2 = column(gain_mid[...], CO)

    def h1_at(f, r):
        H1[f, r] = norm_fwd(XE[f, r].astype(F32), g1).astype(BF16)

    loc[2].wait()
    loc[3].wait()

    def turn(i, _):
        kt, kh, kw = i // 9, (i // 3) % 3, i % 3
        WTI[i] = WIN[kt, kh, kw].astype(F32).T.astype(BF16)
        WTM[i] = WMID[kt, kh, kw].astype(F32).T.astype(BF16)
        return 0

    lax.fori_loop(0, 27, turn, 0)
    loc[0].wait()

    def h1_own(i, _):
        h1_at(2 + i // 2, 1 + i % 2)
        return 0

    lax.fori_loop(0, 8, h1_own, 0)

    loc[1].wait()
    for item in along:
        item.got()
    for f in range(6):
        frame = t * FR + f
        at = jnp.int32(0)
        found = jnp.int32(0)
        for j in range(SC * TM):
            hit = (sf[0, j] == frame).astype(jnp.int32)
            at = jnp.maximum(at, j * hit)
            found = jnp.maximum(found, hit)
        factor = found.astype(F32)
        for r in range(RW):
            CE[f, 1 + r] = (SG[at, r].astype(F32) * factor).astype(BF16)
    cot_halo = [
        Copy(CE.at[:, 2], CE.at[:, 0], dev(hh=h + 1), has_n, has_p),
        Copy(CE.at[:, 1], CE.at[:, 3], dev(hh=h - 1), has_p, has_n),
    ]
    for item in cot_halo:
        item.start()

    skip_a = jnp.zeros((CO, W), F32)
    skip_b = jnp.zeros((CO, W), F32)
    for f in range(FR):
        cot = pair(CE, f, 1)
        xs = pair(XE, 2 + f, 1)
        skip_a = skip_a + dot_nt(cot, xs[:W])
        skip_b = skip_b + dot_nt(cot, jnp.concatenate([jnp.zeros((64, 2 * W), BF16), xs[W:]], axis=0))
    g_mid[pl.ds(2016, 32)] = skip_a[:32].astype(BF16)
    g_in[pl.ds(4032, 64)] = skip_a[32:].astype(BF16)

    for item in x_halo:
        item.got()

    def h1_rows(f, _):
        h1_at(f, 0)
        h1_at(f, 3)
        return 0

    def h1_prior(f, _):
        h1_at(f, 1)
        h1_at(f, 2)
        return 0

    lax.fori_loop(0, 6, h1_rows, 0)
    lax.fori_loop(0, 2, h1_prior, 0)

    def forward(f, _):
        acc = jnp.zeros((3 * CO, 2 * W), F32)
        for kt, kh in TAPS:
            acc = acc + dot(WIN[kt, kh].reshape(3 * CO, CI), pair(H1, f + kt, kh))
        for r in range(RW):
            part = acc[:, r * W:(r + 1) * W]
            a1 = part[CO:2 * CO] + behind(part[:CO]) + ahead(part[2 * CO:])
            a1 = a1.astype(BF16)
            A1[f, r] = a1
            H2[f, r] = norm_fwd(a1.astype(F32), g2).astype(BF16)
        return 0

    lax.fori_loop(0, FR, forward, 0)

    for item in cot_halo:
        item.got()

    def back_mid(f, _):
        acc = jnp.zeros((3 * CO, 2 * W), F32)
        for n, (kt, kh) in enumerate(TAPS):
            acc = acc + dot(WTM[pl.ds(3 * n, 3)].reshape(3 * CO, CO), pair(CE, f + 2 - kt, 2 - kh))
        for r in range(RW):
            part = acc[:, r * W:(r + 1) * W]
            gh2 = part[CO:2 * CO] + ahead(part[:CO]) + behind(part[2 * CO:])
            ga1 = norm_pull(A1[f, r].astype(F32), g2, gh2).astype(BF16)
            GE[f, 1 + r] = ga1
            wide = ga1.astype(F32)
            lanes = pl.ds(r * W, W)
            GS[f, pl.ds(0, CO), lanes] = ahead(wide).astype(BF16)
            GS[f, pl.ds(CO, CO), lanes] = ga1
            GS[f, pl.ds(2 * CO, CO), lanes] = behind(wide).astype(BF16)
        return 0

    lax.fori_loop(0, FR, back_mid, 0)
    ga_halo = [
        Copy(GE.at[pl.ds(0, 4), 2], GE.at[pl.ds(0, 4), 0], dev(hh=h + 1), has_n, has_p),
        Copy(GE.at[pl.ds(0, 4), 1], GE.at[pl.ds(0, 4), 3], dev(hh=h - 1), has_p, has_n),
        Copy(GE.at[pl.ds(0, 2), pl.ds(1, 2)], GE.at[pl.ds(4, 2), pl.ds(1, 2)], dev(tt=t - 1), t_p, t_n),
        Copy(GE.at[pl.ds(0, 2), 2], GE.at[pl.ds(4, 2), 0], dev(tt=t - 1, hh=h + 1),
             both(t_p, has_n), both(t_n, has_p)),
        Copy(GE.at[pl.ds(0, 2), 1], GE.at[pl.ds(4, 2), 3], dev(tt=t - 1, hh=h - 1),
             both(t_p, has_p), both(t_n, has_n)),
    ]
    for item in ga_halo:
        item.start()

    for n, taps in enumerate(PAIRS):
        acc = jnp.zeros((3 * CO, 3 * W), F32)
        for f in range(FR):
            one = [pair(H1, f + TAPS[i][0], TAPS[i][1]) for i in taps]
            rhs = jnp.concatenate([one[0][:W], one[1][:W], one[0][W:], one[1][W:]], axis=0)
            acc = acc + dot_nt(GS[f], rhs)
        for j in range(3):
            g_in[pl.ds(864 * n + 288 * j, 288)] = acc[:, j * W:(j + 1) * W].astype(BF16)
    acc = jnp.zeros((3 * CO, 2 * W), F32)
    for f in range(FR):
        one = pair(H1, f + 2, 2)
        rhs = jnp.concatenate([one, jnp.zeros((64, 2 * W), BF16)], axis=0)
        acc = acc + dot_nt(GS[f], rhs)
    for j in range(2):
        g_in[pl.ds(3456 + 288 * j, 288)] = acc[:, j * W:(j + 1) * W].astype(BF16)

    def reduce(g, rc, s, a1, b1, p, a2, b2, cc, zz, fin, out, rows):
        half = rows // 2
        ha = half // 2
        q = ha // 4
        e = q // 4
        owners = 2 * e // 16
        mine = pl.multiple_of(c * half, half)
        other = pl.multiple_of((1 - c) * half, half)

        def at(off, n):
            return pl.ds(pl.multiple_of(off, 16), n)

        def total(terms):
            out = terms[0].astype(F32)
            for term in terms[1:]:
                out = out + term.astype(F32)
            return out.astype(BF16)

        near = (1, 3, 2)
        far = (2, 1, 3, 0)

        def piece_a(base, k):
            return at(base + (xx + 4 - k) % 4 * q, q)

        def piece_b(base, k):
            return at(base + ha + (y + 4 - k) % 4 * q, q)

        core = []
        for k in far:
            for piece in (piece_a, piece_b):
                core.append(Copy(g.at[piece(other, k)], rc.at[piece(0, k)], dev(cc=1 - c)))
                core[-1].start()
        yield
        one = []
        for k in far[:3]:
            for n, piece in enumerate((piece_a, piece_b)):
                core.pop(0).got()
                s[piece(0, k)] = total([g[piece(mine, k)], rc[piece(0, k)]])
                if n == 0:
                    one.append(Copy(s.at[piece(0, k)], a1.at[k - 1], x_peer((xx + 4 - k) % 4)))
                else:
                    one.append(Copy(s.at[piece(0, k)], b1.at[k - 1], y_peer((y + 4 - k) % 4)))
                one[-1].start()
        for item in core:
            item.got()
        yield
        for item in one:
            item.got()
        p[pl.ds(0, q)] = total([g[piece_a(mine, 0)], rc[piece_a(0, 0)], a1[0], a1[1], a1[2]])
        p[pl.ds(q, q)] = total([g[piece_b(mine, 0)], rc[piece_b(0, 0)], b1[0], b1[1], b1[2]])
        two = []
        for k in (2, 1, 3):
            xp, yp = (xx + k) % 4, (y + k) % 4
            two.append(Copy(p.at[at(yp * e, e)], a2.at[k - 1], y_peer(yp)))
            two.append(Copy(p.at[at(q + xp * e, e)], b2.at[k - 1], x_peer(xp)))
        for item in two:
            item.start()
        yield
        for item in two:
            item.got()
        cc[pl.ds(0, e)] = total([p[at(y * e, e)], a2[0], a2[1], a2[2]])
        cc[pl.ds(e, e)] = total([p[at(q + xx * e, e)], b2[0], b2[1], b2[2]])
        ks = (4, 3, 5, 2, 6, 1, 7)
        own = None if owners == 8 else z < owners
        three = []
        for k in ks:
            zp = (z + k) % 8
            three.append(Copy(cc.at[at(zp % owners * 16, 16)], zz.at[k - 1], z_peer(zp),
                              None if owners == 8 else zp < owners, own))
        for item in three:
            item.start()
        yield
        for item in three:
            item.got()
        chain_b = (z >= owners // 2).astype(jnp.int32)
        zt = z % (owners // 2)
        base_a = mine + xx * q + y * e
        base_b = mine + ha + y * q + xx * e
        place = base_a + chain_b * (base_b - base_a) + zt * 16

        def finish():
            fin[at(place, 16)] = total([cc[at(z % owners * 16, 16)]] + [zz[k] for k in range(7)])

        when(own, finish)
        four = []
        for k in ks:
            zp, zm = (z + k) % 8, (z + 8 - k) % 8
            four.append(Copy(fin.at[at(place, 16)], fin.at[at(place, 16)], z_peer(zp),
                             own, None if owners == 8 else zm < owners))
        for item in four:
            item.start()
        yield
        for item in four:
            item.got()
        def part_a(k):
            return at(mine + xx * q + (y + 4 - k) % 4 * e, e)

        def part_b(k):
            return at(mine + ha + y * q + (xx + 4 - k) % 4 * e, e)

        six = {k: [] for k in near}

        def onward(k):
            for m in (2, 1, 3):
                six[m].append((Copy(fin.at[part_a(k)], fin.at[part_a(k)], x_peer((xx + m) % 4)),
                               Copy(fin.at[part_b(k)], fin.at[part_b(k)], y_peer((y + m) % 4))))
                for item in six[m][-1]:
                    item.start()

        five = {}
        for k in (2, 1, 3):
            five[k] = (Copy(fin.at[part_a(0)], fin.at[part_a(0)], y_peer((y + k) % 4)),
                       Copy(fin.at[part_b(0)], fin.at[part_b(0)], x_peer((xx + k) % 4)))
            for item in five[k]:
                item.start()
        onward(0)
        yield
        for k in near:
            for item in five[k]:
                item.got()
            onward(k)
        last = []

        def deliver(k):
            for piece in (piece_a, piece_b):
                rng = piece(mine, k)
                last.append(Copy(fin.at[rng], out.at[rng], dev(cc=1 - c)))
                last[-1].start()
                keep(fin.at[rng], out.at[rng])

        deliver(0)
        yield
        for m in near:
            for items in six[m]:
                for item in items:
                    item.got()
            deliver(m)
        yield
        for item in last:
            item.got()
        yield

    big = reduce(g_in, rc_in, s_in, a1_in, b1_in, p_in, a2_in, b2_in, c_in, z_in, fin_in, out_in, ROWS_IN)
    small = reduce(g_mid, rc_mid, s_mid, a1_mid, b1_mid, p_mid, a2_mid, b2_mid, c_mid, z_mid, fin_mid, out_mid, ROWS_MID)
    next(big)

    def cot_shift(f, _):
        for r in range(4):
            wide = CE[f, r].astype(F32)
            lanes = pl.ds(r * W, W)
            CS[f, pl.ds(0, CO), lanes] = ahead(wide).astype(BF16)
            CS[f, pl.ds(CO, CO), lanes] = CE[f, r]
            CS[f, pl.ds(2 * CO, CO), lanes] = behind(wide).astype(BF16)
        return 0

    lax.fori_loop(0, 6, cot_shift, 0)

    def cot_window(f, tap):
        kt, kh = TAPS[tap]
        return CS[f + 2 - kt, :, pl.ds((2 - kh) * W, 2 * W)]

    for n in range(2):
        acc = jnp.zeros((CO, 9 * W), F32)
        for f in range(FR):
            rhs = jnp.concatenate([cot_window(f, 4 * n + i) for i in range(4)], axis=0)
            acc = acc + dot_nt(pair(H2, f, 0), rhs)
        for j in range(9):
            g_mid[pl.ds(864 * n + CO * j, CO)] = acc[:, j * W:(j + 1) * W].astype(BF16)
    acc = jnp.zeros((CO, 3 * W), F32)
    for f in range(FR):
        rhs = jnp.concatenate([cot_window(f, 8), jnp.zeros((CO, 2 * W), BF16)], axis=0)
        acc = acc + dot_nt(pair(H2, f, 0), rhs)
    g_mid[pl.ds(1728, CO)] = acc[:, :W].astype(BF16)
    g_mid[pl.ds(1824, CO)] = acc[:, W:2 * W].astype(BF16)
    g_mid[pl.ds(1920, CO)] = (acc[:, 2 * W:] + skip_b).astype(BF16)

    next(small)
    next(big)
    next(small)

    def back_in(f):
        acc = jnp.zeros((3 * CI, 2 * W), F32)
        for n, (kt, kh) in enumerate(TAPS):
            acc = acc + dot(WTI[pl.ds(3 * n, 3)].reshape(3 * CI, CO), pair(GE, f + 2 - kt, 2 - kh))
        skip = lax.dot_general(wskip[...], pair(CE, f, 1), (((0,), (0,)), ((), ())),
                               preferred_element_type=F32)
        for r in range(RW):
            part = acc[:, r * W:(r + 1) * W]
            gh1 = part[CI:2 * CI] + ahead(part[:CI]) + behind(part[2 * CI:])
            grad = norm_pull(XE[2 + f, 1 + r].astype(F32), g1, gh1) + skip[:, r * W:(r + 1) * W]
            OX[f, r] = grad.astype(BF16)

    for item in ga_halo:
        item.got()
    for f in range(FR):
        back_in(f)
        next(big)
        next(small)
    keep(OX, out_x.at[0])
    for _ in range(3):
        next(big)
        next(small)
    for item in sent:
        item.left()
    for item in kept:
        item.wait()


def assemble(scale, gx, fi, fm, out_x, out_in, out_mid, out_skip, BI, BM, BS, sem):
    copies = []

    def put(src, dst):
        copy = pltpu.make_async_copy(src, dst, sem.at[len(copies)])
        copy.start()
        copies.append(copy)

    put(gx, out_x)
    for n, taps in enumerate(PAIRS):
        for kw in range(3):
            low = fi[pl.ds(864 * n + 576 + CO * kw, CO)].astype(F32) * scale
            for j, i in enumerate(taps):
                kt, kh = TAPS[i]
                BI[kt, kh, kw, :, pl.ds(0, W)] = fi[pl.ds(864 * n + 288 * j + CO * kw, CO)].astype(F32) * scale
                rest = low if j == 0 else pltpu.roll(low, 64, 1)
                BI[kt, kh, kw, :, pl.ds(W, 64)] = rest[:, :64]
        for i in taps:
            put(BI.at[TAPS[i]], out_in.at[TAPS[i]])
    for kw in range(3):
        BI[2, 2, kw, :, pl.ds(0, W)] = fi[pl.ds(3456 + CO * kw, CO)].astype(F32) * scale
        BI[2, 2, kw, :, pl.ds(W, 64)] = (fi[pl.ds(3744 + CO * kw, CO)].astype(F32) * scale)[:, :64]
    put(BI.at[2, 2], out_in.at[2, 2])
    tail = fm[pl.ds(1920, CO)].astype(F32) * scale
    BS[pl.ds(0, 32), pl.ds(0, W)] = fm[pl.ds(2016, 32)].astype(F32) * scale
    BS[pl.ds(32, 64), pl.ds(0, W)] = fi[pl.ds(4032, 64)].astype(F32) * scale
    BS[:, pl.ds(W, 64)] = pltpu.roll(tail, 64, 1)[:, :64]
    put(BS, out_skip)
    for j in range(20):
        BM[pl.ds(W * j, W)] = (fm[pl.ds(CO * j, CO)].astype(F32) * scale).T
        if j % 5 == 4:
            rows = pl.ds(W * (j - 4), 5 * W)
            put(BM.at[rows], out_mid.at[rows])
    BM[pl.ds(2560, 32)] = tail.T[:32]
    put(BM.at[pl.ds(2560, 32)], out_mid.at[pl.ds(2560, 32)])
    for copy in copies:
        copy.wait()


def reduce_scratch(rows):
    half = rows // 2
    q, e = half // 8, half // 32
    return {
        "g": (rows, W), "rc": (half, W), "s": (half, W), "a1": (3, q, W), "b1": (3, q, W), "p": (2 * q, W),
        "a2": (3, e, W), "b2": (3, e, W), "c": (2 * e, W), "z": (7, 16, W), "fin": (rows, W),
    }


def shards(inputs, gain_in, conv_in, gain_mid, conv_mid, conv_skip, scored_grads, scored_frames):
    count = scored_frames.shape[1] * inputs.shape[0] * lax.axis_size("dp")
    scale = 1.0 / math.sqrt(count * RW * HT * W)
    vmem = pl.BlockSpec(memory_space=pltpu.VMEM)
    anyw = pl.BlockSpec(memory_space=pl.ANY)
    smem = pl.BlockSpec(memory_space=pltpu.SMEM)
    big, small = reduce_scratch(ROWS_IN), reduce_scratch(ROWS_MID)

    def buf(shape, dtype=BF16):
        return pltpu.VMEM(shape, dtype)

    scratch = [
        buf((FR, RW, CI, W)),
        buf((6, 4, CI, W)), buf((6, 4, CI, W)), buf((SC * TM, RW, CO, W)), buf((6, 4, CO, W)),
        buf((6, 3 * CO, 4 * W)), buf((6, 4, CO, W)), buf((FR, 3 * CO, RW * W)),
        buf((FR, RW, CO, W)), buf((FR, RW, CO, W)),
        buf((3, 3, 3, CO, CI)), buf((3, 3, 3, CO, CO)), buf((27, CI, CO)), buf((27, CO, CO)),
    ]
    for name in ("g", "rc", "s"):
        scratch += [buf(big[name]), buf(small[name])]
    scratch += [buf(big["a1"]), buf(big["b1"]), buf(small["a1"]), buf(small["b1"])]
    scratch += [buf(big["p"]), buf(small["p"])]
    scratch += [buf(big["a2"]), buf(big["b2"]), buf(small["a2"]), buf(small["b2"])]
    for name in ("c", "z", "fin"):
        scratch += [buf(big[name]), buf(small[name])]
    scratch += [
        pltpu.SemaphoreType.DMA((N_SEMS,)), pltpu.SemaphoreType.DMA((N_SEMS,)),
        pltpu.SemaphoreType.DMA((N_LOCAL,)),
    ]

    def body(*refs):
        kernel(scale, *refs)

    grad_x, sum_in, sum_mid = pl.pallas_call(
        body,
        out_shape=(
            jax.ShapeDtypeStruct(inputs.shape, BF16),
            jax.ShapeDtypeStruct((ROWS_IN, W), BF16),
            jax.ShapeDtypeStruct((ROWS_MID, W), BF16),
        ),
        in_specs=[smem, anyw, vmem, anyw, vmem, anyw, vmem, anyw],
        out_specs=(anyw, anyw, anyw),
        scratch_shapes=scratch,
        compiler_params=pltpu.CompilerParams(
            collective_id=0, has_side_effects=True, vmem_limit_bytes=63 * 1024 * 1024
        ),
        name="block_backward",
    )(scored_frames, inputs, gain_in[None, :], conv_in, gain_mid[None, :], conv_mid, conv_skip, scored_grads)

    def last(*refs):
        assemble(scale, *refs)

    grad_inputs, grad_in, grad_mid, grad_skip = pl.pallas_call(
        last,
        out_shape=(
            jax.ShapeDtypeStruct(inputs.shape, BF16),
            jax.ShapeDtypeStruct(conv_in.shape, F32),
            jax.ShapeDtypeStruct((27 * CO, CO), F32),
            jax.ShapeDtypeStruct(conv_skip.shape, F32),
        ),
        in_specs=[vmem, vmem, vmem],
        out_specs=(anyw, anyw, anyw, anyw),
        scratch_shapes=[
            buf(conv_in.shape, F32), buf((27 * CO, CO), F32), buf(conv_skip.shape, F32),
            pltpu.SemaphoreType.DMA((16,)),
        ],
        compiler_params=pltpu.CompilerParams(vmem_limit_bytes=63 * 1024 * 1024),
        name="assemble",
    )(grad_x, sum_in, sum_mid)
    return grad_inputs, grad_in, grad_mid.reshape(conv_mid.shape), grad_skip


def solution(mesh):
    in_specs = (
        P("dp", "tm", "height", None, None),
        P(),
        P(),
        P(),
        P(),
        P(),
        P("dp", "tm", "height", None, None),
        P("dp", None),
    )
    out_specs = (P("dp", "tm", "height", None, None), P(), P(), P())
    return jax.shard_map(shards, mesh=mesh, in_specs=in_specs, out_specs=out_specs, check_vma=False)
```

```python
import math

import jax
import jax.numpy as jnp
from jax import lax
from jax.experimental import pallas as pl
from jax.experimental.pallas import tpu as pltpu
from jax.sharding import PartitionSpec as P

MESH = pl.DeviceIdType.MESH
F32 = jnp.float32
BF16 = jnp.bfloat16
FR, RW, CI, CO, W = 4, 2, 192, 96, 128
TM, HT = 8, 16
SC = 2
EPS = 1e-06
TAPS = [(kt, kh) for kt in range(3) for kh in range(3)]
PAIRS = [(0, 1), (2, 3), (4, 5), (6, 7)]
ROWS_IN, ROWS_MID = 4096, 2048


def sigmoid(u):
    return 1.0 / (1.0 + jnp.exp(-u))


def norm_parts(v, g):
    s = lax.rsqrt(jnp.mean(v * v, axis=0, keepdims=True) + EPS)
    n = v * s
    u = n * g
    return s, n, u, sigmoid(u)


def norm_fwd(v, g):
    _, _, u, sg = norm_parts(v, g)
    return u * sg


def norm_pull(v, g, ct):
    s, n, u, sg = norm_parts(v, g)
    dn = ct * (sg * (1.0 + u * (1.0 - sg))) * g
    return s * (dn - n * jnp.mean(dn * n, axis=0, keepdims=True))


def ahead(v):
    lane = lax.broadcasted_iota(jnp.int32, v.shape, 1)
    return jnp.where(lane == W - 1, 0.0, pltpu.roll(v, W - 1, 1))


def behind(v):
    lane = lax.broadcasted_iota(jnp.int32, v.shape, 1)
    return jnp.where(lane == 0, 0.0, pltpu.roll(v, 1, 1))


def column(row, n):
    r = lax.broadcasted_iota(jnp.int32, (n, n), 0)
    c = lax.broadcasted_iota(jnp.int32, (n, n), 1)
    return jnp.sum(jnp.where(r == c, jnp.broadcast_to(row, (n, n)), 0.0), axis=1, keepdims=True)


def dot(a, b):
    return jnp.dot(a, b, preferred_element_type=F32)


def dot_nt(a, b):
    return lax.dot_general(a, b, (((1,), (1,)), ((), ())), preferred_element_type=F32)


def pair(ref, f, r):
    return jnp.concatenate([ref[f, r], ref[f, r + 1]], axis=1)


class Sems:
    def __init__(self, send, recv):
        self.send, self.recv, self.n = send, recv, 0

    def take(self, count):
        at = self.n
        self.n += count
        return list(range(at, at + count))


N_SEMS = 192
N_LOCAL = 24


def when(cond, fn):
    if cond is None:
        fn()
    else:
        pl.when(cond)(fn)


def kernel(scale, sf, x_hbm, gain_in, win_hbm, gain_mid, wmid_hbm, wskip, sg_hbm,
           out_x, out_in, out_mid,
           OX,           XE, H1, SG, CE, CS, GE, GS, ACC, A1, H2, WIN, WMID, WTI, WTM,
           g_in, g_mid, rc_in, rc_mid, s_in, s_mid,
           a1_in, b1_in, a1_mid, b1_mid, p_in, p_mid, a2_in, b2_in, a2_mid, b2_mid,
           c_in, c_mid, z_in, z_mid, fin_in, fin_mid,
           send, recv, local):
    c = lax.axis_index("dp")
    t = lax.axis_index("tm")
    h = lax.axis_index("height")
    y, x_lo = t % 4, t // 4
    z, x_hi = h // 2, h % 2
    xx = x_hi * 2 + x_lo
    sems = Sems(send, recv)
    sent = []

    def dev(tt=None, hh=None, cc=None):
        d = {}
        d["dp"] = c if cc is None else cc
        d["tm"] = t if tt is None else tt
        d["height"] = h if hh is None else hh
        return d

    def x_peer(v):
        return dev(tt=y + 4 * (v % 2), hh=z * 2 + v // 2)

    def y_peer(v):
        return dev(tt=x_lo * 4 + v)

    def z_peer(v):
        return dev(hh=v * 2 + x_hi)

    kept = []

    def keep(src, dst):
        copy = pltpu.make_async_copy(src, dst, local.at[4 + len(kept)])
        copy.start()
        kept.append(copy)

    class Copy:
        def __init__(self, src, dst, to, s_if=None, r_if=None):
            i = sems.take(1)[0]
            self.d = pltpu.make_async_remote_copy(
                src_ref=src, dst_ref=dst, send_sem=send.at[i], recv_sem=recv.at[i],
                device_id=to, device_id_type=MESH)
            self.s_if, self.r_if = s_if, r_if

        def start(self):
            when(self.s_if, lambda: self.d.start())
            sent.append(self)

        def got(self):
            when(self.r_if, lambda: self.d.wait_recv())

        def left(self):
            when(self.s_if, lambda: self.d.wait_send())

    loc = [
        pltpu.make_async_copy(x_hbm.at[0], XE.at[pl.ds(2, FR), pl.ds(1, RW)], local.at[0]),
        pltpu.make_async_copy(sg_hbm.at[0], SG.at[pl.ds(SC * t, SC)], local.at[1]),
        pltpu.make_async_copy(win_hbm, WIN, local.at[2]),
        pltpu.make_async_copy(wmid_hbm, WMID, local.at[3]),
    ]
    for item in loc:
        item.start()

    barrier = pltpu.get_barrier_semaphore()
    friends = [dev(hh=(h + k) % HT) for k in (8, 6, 10, 4, 12, 2, 14, 1, 15)]
    friends += [dev(tt=(t + a) % TM, hh=(h + b) % HT) for a in (1, 7) for b in (1, 15)]
    friends += [y_peer((y + k) % 4) for k in (1, 2, 3)]
    friends += [dev(tt=(t + k) % TM) for k in (1, 7, 4)]
    friends += [x_peer(3 - xx), dev(cc=1 - c)]
    for to in friends:
        pl.semaphore_signal(barrier, inc=1, device_id=to, device_id_type=MESH)

    first_t, last_t, first_h, last_h = t == 0, t == TM - 1, h == 0, h == HT - 1

    def zero(ref, f0, nf, r0, nr, ch):
        def body():
            for f in range(f0, f0 + nf):
                for r in range(r0, r0 + nr):
                    ref[f, r] = jnp.zeros((ch, W), BF16)
        return body

    pl.when(first_t)(zero(XE, 0, 2, 0, 4, CI))
    pl.when(jnp.logical_and(first_h, t > 0))(zero(XE, 0, 2, 0, 1, CI))
    pl.when(jnp.logical_and(last_h, t > 0))(zero(XE, 0, 2, 3, 1, CI))
    pl.when(first_h)(zero(XE, 2, 4, 0, 1, CI))
    pl.when(last_h)(zero(XE, 2, 4, 3, 1, CI))
    pl.when(first_h)(zero(CE, 0, 6, 0, 1, CO))
    pl.when(last_h)(zero(CE, 0, 6, 3, 1, CO))
    pl.when(last_t)(zero(GE, 4, 2, 0, 4, CO))
    pl.when(jnp.logical_and(first_h, t < TM - 1))(zero(GE, 4, 2, 0, 1, CO))
    pl.when(jnp.logical_and(last_h, t < TM - 1))(zero(GE, 4, 2, 3, 1, CO))
    pl.when(first_h)(zero(GE, 0, 4, 0, 1, CO))
    pl.when(last_h)(zero(GE, 0, 4, 3, 1, CO))

    pl.semaphore_wait(barrier, len(friends))

    both = jnp.logical_and
    has_n, has_p = h < HT - 1, h > 0
    t_n, t_p = t < TM - 1, t > 0

    other_t = (t + TM // 2) % TM
    across = [Copy(sg_hbm.at[0, j], SG.at[SC * t + j], dev(tt=other_t)) for j in range(SC)]
    along = [Copy(sg_hbm.at[0], SG.at[pl.ds(SC * t, SC)], y_peer((y + k) % 4)) for k in (1, 3, 2)]
    for item in across + along:
        item.start()

    src = x_hbm.at[0]
    x_halo = [
        Copy(src.at[:, 1], XE.at[pl.ds(2, 4), 0], dev(hh=h + 1), has_n, has_p),
        Copy(src.at[:, 0], XE.at[pl.ds(2, 4), 3], dev(hh=h - 1), has_p, has_n),
        Copy(src.at[pl.ds(2, 2)], XE.at[pl.ds(0, 2), pl.ds(1, 2)], dev(tt=t + 1), t_n, t_p),
        Copy(src.at[pl.ds(2, 2), 1], XE.at[pl.ds(0, 2), 0], dev(tt=t + 1, hh=h + 1),
             both(t_n, has_n), both(t_p, has_p)),
        Copy(src.at[pl.ds(2, 2), 0], XE.at[pl.ds(0, 2), 3], dev(tt=t + 1, hh=h - 1),
             both(t_n, has_p), both(t_p, has_n)),
    ]
    for item in x_halo[:2]:
        item.start()

    for j in range(SC):
        across[j].got()
        at_j = SC * other_t + j
        onward = [Copy(SG.at[at_j], SG.at[at_j], y_peer((y + k) % 4)) for k in (1, 3, 2)]
        for item in onward:
            item.start()
        along += onward
    for item in x_halo[2:]:
        item.start()

    g1 = column(gain_in[...], CI)
    g2 = column(gain_mid[...], CO)

    def h1_at(f, r):
        H1[f, r] = norm_fwd(XE[f, r].astype(F32), g1).astype(BF16)

    loc[2].wait()
    loc[3].wait()

    def turn(i, _):
        kt, kh, kw = i // 9, (i // 3) % 3, i % 3
        WTI[i] = WIN[kt, kh, kw].astype(F32).T.astype(BF16)
        WTM[i] = WMID[kt, kh, kw].astype(F32).T.astype(BF16)
        return 0

    lax.fori_loop(0, 27, turn, 0)
    loc[0].wait()

    def h1_own(i, _):
        h1_at(2 + i // 2, 1 + i % 2)
        return 0

    lax.fori_loop(0, 8, h1_own, 0)

    loc[1].wait()
    for item in along:
        item.got()
    for f in range(6):
        frame = t * FR + f
        at = jnp.int32(0)
        found = jnp.int32(0)
        for j in range(SC * TM):
            hit = (sf[0, j] == frame).astype(jnp.int32)
            at = jnp.maximum(at, j * hit)
            found = jnp.maximum(found, hit)
        factor = found.astype(F32)
        for r in range(RW):
            CE[f, 1 + r] = (SG[at, r].astype(F32) * factor).astype(BF16)
    cot_halo = [
        Copy(CE.at[:, 2], CE.at[:, 0], dev(hh=h + 1), has_n, has_p),
        Copy(CE.at[:, 1], CE.at[:, 3], dev(hh=h - 1), has_p, has_n),
    ]
    for item in cot_halo:
        item.start()

    skip_a = jnp.zeros((CO, W), F32)
    skip_b = jnp.zeros((CO, W), F32)
    for f in range(FR):
        cot = pair(CE, f, 1)
        xs = pair(XE, 2 + f, 1)
        skip_a = skip_a + dot_nt(cot, xs[:W])
        skip_b = skip_b + dot_nt(cot, jnp.concatenate([jnp.zeros((64, 2 * W), BF16), xs[W:]], axis=0))
    g_mid[pl.ds(2016, 32)] = skip_a[:32].astype(BF16)
    g_in[pl.ds(2016, 32)] = skip_a[32:64].astype(BF16)
    g_in[pl.ds(4064, 32)] = skip_a[64:].astype(BF16)

    def mid_part(g, r, khs):
        acc = jnp.zeros((3 * CO, 2 * W), F32)
        for kt in range(3):
            for kh in khs:
                f, row = 2 * g + 2 - kt, r + 2 - kh
                matrix = WTM[pl.ds(9 * kt + 3 * kh, 3)].reshape(3 * CO, CO)
                acc = acc + dot(matrix, jnp.concatenate([CE[f, row], CE[f + 1, row]], axis=1))
        return acc

    def own_mid(g, _):
        ACC[g, 0] = mid_part(g, 0, (0, 1))
        ACC[g, 1] = mid_part(g, 1, (1, 2))
        return 0

    lax.fori_loop(0, 2, own_mid, 0)

    for item in x_halo:
        item.got()

    def h1_rows(f, _):
        h1_at(f, 0)
        h1_at(f, 3)
        return 0

    def h1_prior(f, _):
        h1_at(f, 1)
        h1_at(f, 2)
        return 0

    lax.fori_loop(0, 6, h1_rows, 0)
    lax.fori_loop(0, 2, h1_prior, 0)

    def forward(f, _):
        acc = jnp.zeros((3 * CO, 2 * W), F32)
        for kt, kh in TAPS:
            acc = acc + dot(WIN[kt, kh].reshape(3 * CO, CI), pair(H1, f + kt, kh))
        for r in range(RW):
            part = acc[:, r * W:(r + 1) * W]
            a1 = part[CO:2 * CO] + behind(part[:CO]) + ahead(part[2 * CO:])
            a1 = a1.astype(BF16)
            A1[f, r] = a1
            H2[f, r] = norm_fwd(a1.astype(F32), g2).astype(BF16)
        return 0

    lax.fori_loop(0, FR, forward, 0)

    for item in cot_halo:
        item.got()

    def back_mid(g, _):
        for r in range(RW):
            acc = ACC[g, r] + mid_part(g, r, (2,) if r == 0 else (0,))
            for j in range(2):
                f = 2 * g + j
                part = acc[:, j * W:(j + 1) * W]
                gh2 = part[CO:2 * CO] + ahead(part[:CO]) + behind(part[2 * CO:])
                ga1 = norm_pull(A1[f, r].astype(F32), g2, gh2).astype(BF16)
                GE[f, 1 + r] = ga1
                wide = ga1.astype(F32)
                lanes = pl.ds(r * W, W)
                GS[f, pl.ds(0, CO), lanes] = ahead(wide).astype(BF16)
                GS[f, pl.ds(CO, CO), lanes] = ga1
                GS[f, pl.ds(2 * CO, CO), lanes] = behind(wide).astype(BF16)
        return 0

    lax.fori_loop(0, 2, back_mid, 0)
    ga_halo = [
        Copy(GE.at[pl.ds(0, 4), 2], GE.at[pl.ds(0, 4), 0], dev(hh=h + 1), has_n, has_p),
        Copy(GE.at[pl.ds(0, 4), 1], GE.at[pl.ds(0, 4), 3], dev(hh=h - 1), has_p, has_n),
        Copy(GE.at[pl.ds(0, 2), pl.ds(1, 2)], GE.at[pl.ds(4, 2), pl.ds(1, 2)], dev(tt=t - 1), t_p, t_n),
        Copy(GE.at[pl.ds(0, 2), 2], GE.at[pl.ds(4, 2), 0], dev(tt=t - 1, hh=h + 1),
             both(t_p, has_n), both(t_n, has_p)),
        Copy(GE.at[pl.ds(0, 2), 1], GE.at[pl.ds(4, 2), 3], dev(tt=t - 1, hh=h - 1),
             both(t_p, has_p), both(t_n, has_n)),
    ]
    for item in ga_halo:
        item.start()

    def reduce(g, rc, s, a1, b1, p, a2, b2, cc, zz, fin, out, rows, parts=None):
        half = rows // 2
        ha = half // 2
        q = ha // 4
        e = q // 4
        owners = 2 * e // 16
        mine = pl.multiple_of(c * half, half)
        other = pl.multiple_of((1 - c) * half, half)

        def at(off, n):
            return pl.ds(pl.multiple_of(off, 16), n)

        def total(terms):
            out = terms[0].astype(F32)
            for term in terms[1:]:
                out = out + term.astype(F32)
            return out.astype(BF16)

        near = (1, 3, 2)
        far = (2, 1, 3, 0)

        def piece_a(base, k):
            return at(base + (xx + 4 - k) % 4 * q, q)

        def piece_b(base, k):
            return at(base + ha + (y + 4 - k) % 4 * q, q)

        core = []
        if parts:
            for off, n in parts:
                core.append(Copy(g.at[at(other + off, n)], rc.at[pl.ds(off, n)], dev(cc=1 - c)))
                core[-1].start()
                yield
            for item in core:
                item.got()
            core = []
        else:
            for k in far:
                for piece in (piece_a, piece_b):
                    core.append(Copy(g.at[piece(other, k)], rc.at[piece(0, k)], dev(cc=1 - c)))
                    core[-1].start()
            yield
        one = []
        for k in far[:3]:
            for n, piece in enumerate((piece_a, piece_b)):
                if core:
                    core.pop(0).got()
                s[piece(0, k)] = total([g[piece(mine, k)], rc[piece(0, k)]])
                if n == 0:
                    one.append(Copy(s.at[piece(0, k)], a1.at[k - 1], x_peer((xx + 4 - k) % 4)))
                else:
                    one.append(Copy(s.at[piece(0, k)], b1.at[k - 1], y_peer((y + 4 - k) % 4)))
                one[-1].start()
        for item in core:
            item.got()
        yield
        for item in one:
            item.got()
        p[pl.ds(0, q)] = total([g[piece_a(mine, 0)], rc[piece_a(0, 0)], a1[0], a1[1], a1[2]])
        p[pl.ds(q, q)] = total([g[piece_b(mine, 0)], rc[piece_b(0, 0)], b1[0], b1[1], b1[2]])
        two = []
        for k in (2, 1, 3):
            xp, yp = (xx + k) % 4, (y + k) % 4
            two.append(Copy(p.at[at(yp * e, e)], a2.at[k - 1], y_peer(yp)))
            two.append(Copy(p.at[at(q + xp * e, e)], b2.at[k - 1], x_peer(xp)))
        for item in two:
            item.start()
        yield
        for item in two:
            item.got()
        cc[pl.ds(0, e)] = total([p[at(y * e, e)], a2[0], a2[1], a2[2]])
        cc[pl.ds(e, e)] = total([p[at(q + xx * e, e)], b2[0], b2[1], b2[2]])
        ks = (4, 3, 5, 2, 6, 1, 7)
        own = None if owners == 8 else z < owners
        three = []
        for k in ks:
            zp = (z + k) % 8
            three.append(Copy(cc.at[at(zp % owners * 16, 16)], zz.at[k - 1], z_peer(zp),
                              None if owners == 8 else zp < owners, own))
        for item in three:
            item.start()
        yield
        for item in three:
            item.got()
        chain_b = (z >= owners // 2).astype(jnp.int32)
        zt = z % (owners // 2)
        base_a = mine + xx * q + y * e
        base_b = mine + ha + y * q + xx * e
        place = base_a + chain_b * (base_b - base_a) + zt * 16

        def finish():
            fin[at(place, 16)] = total([cc[at(z % owners * 16, 16)]] + [zz[k] for k in range(7)])

        when(own, finish)
        four = []
        for k in ks:
            zp, zm = (z + k) % 8, (z + 8 - k) % 8
            four.append(Copy(fin.at[at(place, 16)], fin.at[at(place, 16)], z_peer(zp),
                             own, None if owners == 8 else zm < owners))
        for item in four:
            item.start()
        yield
        for item in four:
            item.got()
        def part_a(k):
            return at(mine + xx * q + (y + 4 - k) % 4 * e, e)

        def part_b(k):
            return at(mine + ha + y * q + (xx + 4 - k) % 4 * e, e)

        six = {k: [] for k in near}

        def onward(k):
            for m in (2, 1, 3):
                six[m].append((Copy(fin.at[part_a(k)], fin.at[part_a(k)], x_peer((xx + m) % 4)),
                               Copy(fin.at[part_b(k)], fin.at[part_b(k)], y_peer((y + m) % 4))))
                for item in six[m][-1]:
                    item.start()

        five = {}
        for k in (2, 1, 3):
            five[k] = (Copy(fin.at[part_a(0)], fin.at[part_a(0)], y_peer((y + k) % 4)),
                       Copy(fin.at[part_b(0)], fin.at[part_b(0)], x_peer((xx + k) % 4)))
            for item in five[k]:
                item.start()
        onward(0)
        yield
        for k in near:
            for item in five[k]:
                item.got()
            onward(k)
        last = []

        def deliver(k):
            for piece in (piece_a, piece_b):
                rng = piece(mine, k)
                last.append(Copy(fin.at[rng], out.at[rng], dev(cc=1 - c)))
                last[-1].start()
                keep(fin.at[rng], out.at[rng])

        deliver(0)
        yield
        for m in near:
            for items in six[m]:
                for item in items:
                    item.got()
            deliver(m)
        yield
        for item in last:
            item.got()
        yield

    big = reduce(g_in, rc_in, s_in, a1_in, b1_in, p_in, a2_in, b2_in, c_in, z_in, fin_in, out_in, ROWS_IN,
                 [(432 * n, 432) for n in range(4)] + [(1728, 320)])
    small = reduce(g_mid, rc_mid, s_mid, a1_mid, b1_mid, p_mid, a2_mid, b2_mid, c_mid, z_mid, fin_mid, out_mid, ROWS_MID)
    for n, taps in enumerate(PAIRS):
        acc = jnp.zeros((3 * CO, 3 * W), F32)
        for f in range(FR):
            one = [pair(H1, f + TAPS[i][0], TAPS[i][1]) for i in taps]
            rhs = jnp.concatenate([one[0][:W], one[1][:W], one[0][W:], one[1][W:]], axis=0)
            acc = acc + dot_nt(GS[f], rhs)
        blocks = [acc[:, j * W:(j + 1) * W].astype(BF16) for j in range(3)]
        g_in[pl.ds(432 * n, 288)] = blocks[0]
        g_in[pl.ds(432 * n + 288, 144)] = blocks[1][:144]
        g_in[pl.ds(2048 + 432 * n, 144)] = blocks[1][144:]
        g_in[pl.ds(2048 + 432 * n + 144, 288)] = blocks[2]
        next(big)
    acc = jnp.zeros((3 * CO, 2 * W), F32)
    for f in range(FR):
        rhs = jnp.concatenate([pair(H1, f + 2, 2), jnp.zeros((64, 2 * W), BF16)], axis=0)
        acc = acc + dot_nt(GS[f], rhs)
    for j in range(2):
        g_in[pl.ds(2048 * j + 1728, 288)] = acc[:, j * W:(j + 1) * W].astype(BF16)
    next(big)

    def cot_shift(f, _):
        for r in range(4):
            wide = CE[f, r].astype(F32)
            lanes = pl.ds(r * W, W)
            CS[f, pl.ds(0, CO), lanes] = ahead(wide).astype(BF16)
            CS[f, pl.ds(CO, CO), lanes] = CE[f, r]
            CS[f, pl.ds(2 * CO, CO), lanes] = behind(wide).astype(BF16)
        return 0

    lax.fori_loop(0, 6, cot_shift, 0)

    def cot_window(f, tap):
        kt, kh = TAPS[tap]
        return CS[f + 2 - kt, :, pl.ds((2 - kh) * W, 2 * W)]

    for n in range(2):
        acc = jnp.zeros((CO, 9 * W), F32)
        for f in range(FR):
            rhs = jnp.concatenate([cot_window(f, 4 * n + i) for i in range(4)], axis=0)
            acc = acc + dot_nt(pair(H2, f, 0), rhs)
        for j in range(9):
            g_mid[pl.ds(864 * n + CO * j, CO)] = acc[:, j * W:(j + 1) * W].astype(BF16)
    acc = jnp.zeros((CO, 3 * W), F32)
    for f in range(FR):
        rhs = jnp.concatenate([cot_window(f, 8), jnp.zeros((CO, 2 * W), BF16)], axis=0)
        acc = acc + dot_nt(pair(H2, f, 0), rhs)
    g_mid[pl.ds(1728, CO)] = acc[:, :W].astype(BF16)
    g_mid[pl.ds(1824, CO)] = acc[:, W:2 * W].astype(BF16)
    g_mid[pl.ds(1920, CO)] = (acc[:, 2 * W:] + skip_b).astype(BF16)

    next(small)
    next(big)
    next(small)

    def back_in(f):
        acc = jnp.zeros((3 * CI, 2 * W), F32)
        for n, (kt, kh) in enumerate(TAPS):
            acc = acc + dot(WTI[pl.ds(3 * n, 3)].reshape(3 * CI, CO), pair(GE, f + 2 - kt, 2 - kh))
        skip = lax.dot_general(wskip[...], pair(CE, f, 1), (((0,), (0,)), ((), ())),
                               preferred_element_type=F32)
        for r in range(RW):
            part = acc[:, r * W:(r + 1) * W]
            gh1 = part[CI:2 * CI] + ahead(part[:CI]) + behind(part[2 * CI:])
            grad = norm_pull(XE[2 + f, 1 + r].astype(F32), g1, gh1) + skip[:, r * W:(r + 1) * W]
            OX[f, r] = grad.astype(BF16)

    for item in ga_halo:
        item.got()
    for f in range(FR):
        back_in(f)
        next(big)
        next(small)
    keep(OX, out_x.at[0])
    for _ in range(3):
        next(big)
        next(small)
    for item in sent:
        item.left()
    for item in kept:
        item.wait()


def assemble(scale, gx, fi, fm, out_x, out_in, out_mid, out_skip, BI, BM, BS, sem):
    copies = []

    def put(src, dst):
        copy = pltpu.make_async_copy(src, dst, sem.at[len(copies)])
        copy.start()
        copies.append(copy)

    def rows(n, at, count):
        if at + count <= 432:
            value = fi[pl.ds(432 * n + at, count)]
        elif at >= 432:
            value = fi[pl.ds(2048 + 432 * n + at - 432, count)]
        else:
            cut = 432 - at
            value = jnp.concatenate([fi[pl.ds(432 * n + at, cut)], fi[pl.ds(2048 + 432 * n, count - cut)]], axis=0)
        return value.astype(F32) * scale

    put(gx, out_x)
    for n, taps in enumerate(PAIRS):
        for kw in range(3):
            low = rows(n, 576 + CO * kw, CO)
            for j, i in enumerate(taps):
                kt, kh = TAPS[i]
                BI[kt, kh, kw, :, pl.ds(0, W)] = rows(n, 288 * j + CO * kw, CO)
                rest = low if j == 0 else pltpu.roll(low, 64, 1)
                BI[kt, kh, kw, :, pl.ds(W, 64)] = rest[:, :64]
        for i in taps:
            put(BI.at[TAPS[i]], out_in.at[TAPS[i]])
    for kw in range(3):
        BI[2, 2, kw, :, pl.ds(0, W)] = fi[pl.ds(1728 + CO * kw, CO)].astype(F32) * scale
        BI[2, 2, kw, :, pl.ds(W, 64)] = (fi[pl.ds(3776 + CO * kw, CO)].astype(F32) * scale)[:, :64]
    put(BI.at[2, 2], out_in.at[2, 2])
    tail = fm[pl.ds(1920, CO)].astype(F32) * scale
    BS[pl.ds(0, 32), pl.ds(0, W)] = fm[pl.ds(2016, 32)].astype(F32) * scale
    BS[pl.ds(32, 32), pl.ds(0, W)] = fi[pl.ds(2016, 32)].astype(F32) * scale
    BS[pl.ds(64, 32), pl.ds(0, W)] = fi[pl.ds(4064, 32)].astype(F32) * scale
    BS[:, pl.ds(W, 64)] = pltpu.roll(tail, 64, 1)[:, :64]
    put(BS, out_skip)
    for j in range(20):
        BM[pl.ds(W * j, W)] = (fm[pl.ds(CO * j, CO)].astype(F32) * scale).T
        if j % 5 == 4:
            rows = pl.ds(W * (j - 4), 5 * W)
            put(BM.at[rows], out_mid.at[rows])
    BM[pl.ds(2560, 32)] = tail.T[:32]
    put(BM.at[pl.ds(2560, 32)], out_mid.at[pl.ds(2560, 32)])
    for copy in copies:
        copy.wait()


def reduce_scratch(rows):
    half = rows // 2
    q, e = half // 8, half // 32
    return {
        "g": (rows, W), "rc": (half, W), "s": (half, W), "a1": (3, q, W), "b1": (3, q, W), "p": (2 * q, W),
        "a2": (3, e, W), "b2": (3, e, W), "c": (2 * e, W), "z": (7, 16, W), "fin": (rows, W),
    }


def shards(inputs, gain_in, conv_in, gain_mid, conv_mid, conv_skip, scored_grads, scored_frames):
    count = scored_frames.shape[1] * inputs.shape[0] * lax.axis_size("dp")
    scale = 1.0 / math.sqrt(count * RW * HT * W)
    vmem = pl.BlockSpec(memory_space=pltpu.VMEM)
    anyw = pl.BlockSpec(memory_space=pl.ANY)
    smem = pl.BlockSpec(memory_space=pltpu.SMEM)
    big, small = reduce_scratch(ROWS_IN), reduce_scratch(ROWS_MID)

    def buf(shape, dtype=BF16):
        return pltpu.VMEM(shape, dtype)

    scratch = [
        buf((FR, RW, CI, W)),
        buf((6, 4, CI, W)), buf((6, 4, CI, W)), buf((SC * TM, RW, CO, W)), buf((6, 4, CO, W)),
        buf((6, 3 * CO, 4 * W)), buf((6, 4, CO, W)), buf((FR, 3 * CO, RW * W)), buf((2, RW, 3 * CO, 2 * W), F32),
        buf((FR, RW, CO, W)), buf((FR, RW, CO, W)),
        buf((3, 3, 3, CO, CI)), buf((3, 3, 3, CO, CO)), buf((27, CI, CO)), buf((27, CO, CO)),
    ]
    for name in ("g", "rc", "s"):
        scratch += [buf(big[name]), buf(small[name])]
    scratch += [buf(big["a1"]), buf(big["b1"]), buf(small["a1"]), buf(small["b1"])]
    scratch += [buf(big["p"]), buf(small["p"])]
    scratch += [buf(big["a2"]), buf(big["b2"]), buf(small["a2"]), buf(small["b2"])]
    for name in ("c", "z", "fin"):
        scratch += [buf(big[name]), buf(small[name])]
    scratch += [
        pltpu.SemaphoreType.DMA((N_SEMS,)), pltpu.SemaphoreType.DMA((N_SEMS,)),
        pltpu.SemaphoreType.DMA((N_LOCAL,)),
    ]

    def body(*refs):
        kernel(scale, *refs)

    grad_x, sum_in, sum_mid = pl.pallas_call(
        body,
        out_shape=(
            jax.ShapeDtypeStruct(inputs.shape, BF16),
            jax.ShapeDtypeStruct((ROWS_IN, W), BF16),
            jax.ShapeDtypeStruct((ROWS_MID, W), BF16),
        ),
        in_specs=[smem, anyw, vmem, anyw, vmem, anyw, vmem, anyw],
        out_specs=(anyw, anyw, anyw),
        scratch_shapes=scratch,
        compiler_params=pltpu.CompilerParams(
            collective_id=0, has_side_effects=True, vmem_limit_bytes=63 * 1024 * 1024
        ),
        name="block_backward",
    )(scored_frames, inputs, gain_in[None, :], conv_in, gain_mid[None, :], conv_mid, conv_skip, scored_grads)

    def last(*refs):
        assemble(scale, *refs)

    grad_inputs, grad_in, grad_mid, grad_skip = pl.pallas_call(
        last,
        out_shape=(
            jax.ShapeDtypeStruct(inputs.shape, BF16),
            jax.ShapeDtypeStruct(conv_in.shape, F32),
            jax.ShapeDtypeStruct((27 * CO, CO), F32),
            jax.ShapeDtypeStruct(conv_skip.shape, F32),
        ),
        in_specs=[vmem, vmem, vmem],
        out_specs=(anyw, anyw, anyw, anyw),
        scratch_shapes=[
            buf(conv_in.shape, F32), buf((27 * CO, CO), F32), buf(conv_skip.shape, F32),
            pltpu.SemaphoreType.DMA((16,)),
        ],
        compiler_params=pltpu.CompilerParams(vmem_limit_bytes=63 * 1024 * 1024),
        name="assemble",
    )(grad_x, sum_in, sum_mid)
    return grad_inputs, grad_in, grad_mid.reshape(conv_mid.shape), grad_skip


def solution(mesh):
    in_specs = (
        P("dp", "tm", "height", None, None),
        P(),
        P(),
        P(),
        P(),
        P(),
        P("dp", "tm", "height", None, None),
        P("dp", None),
    )
    out_specs = (P("dp", "tm", "height", None, None), P(), P(), P())
    return jax.shard_map(shards, mesh=mesh, in_specs=in_specs, out_specs=out_specs, check_vma=False)
```

```python
import math

import jax
import jax.numpy as jnp
from jax import lax
from jax.experimental import pallas as pl
from jax.experimental.pallas import tpu as pltpu
from jax.sharding import PartitionSpec as P

MESH = pl.DeviceIdType.MESH
F32 = jnp.float32
BF16 = jnp.bfloat16
FR, RW, CI, CO, W = 4, 2, 192, 96, 128
TM, HT = 8, 16
SC = 2
EPS = 1e-06
TAPS = [(kt, kh) for kt in range(3) for kh in range(3)]
PAIRS = [(0, 1), (2, 3), (4, 5), (6, 7)]
ROWS_IN, ROWS_MID = 4096, 2048


def sigmoid(u):
    return 1.0 / (1.0 + jnp.exp(-u))


def norm_parts(v, g):
    s = lax.rsqrt(jnp.mean(v * v, axis=0, keepdims=True) + EPS)
    n = v * s
    u = n * g
    return s, n, u, sigmoid(u)


def norm_fwd(v, g):
    _, _, u, sg = norm_parts(v, g)
    return u * sg


def norm_pull(v, g, ct):
    s, n, u, sg = norm_parts(v, g)
    dn = ct * (sg * (1.0 + u * (1.0 - sg))) * g
    return s * (dn - n * jnp.mean(dn * n, axis=0, keepdims=True))


def ahead(v):
    lane = lax.broadcasted_iota(jnp.int32, v.shape, 1)
    return jnp.where(lane == W - 1, 0.0, pltpu.roll(v, W - 1, 1))


def behind(v):
    lane = lax.broadcasted_iota(jnp.int32, v.shape, 1)
    return jnp.where(lane == 0, 0.0, pltpu.roll(v, 1, 1))


def column(row, n):
    r = lax.broadcasted_iota(jnp.int32, (n, n), 0)
    c = lax.broadcasted_iota(jnp.int32, (n, n), 1)
    return jnp.sum(jnp.where(r == c, jnp.broadcast_to(row, (n, n)), 0.0), axis=1, keepdims=True)


def dot(a, b):
    return jnp.dot(a, b, preferred_element_type=F32)


def dot_nt(a, b):
    return lax.dot_general(a, b, (((1,), (1,)), ((), ())), preferred_element_type=F32)


def pair(ref, f, r):
    return jnp.concatenate([ref[f, r], ref[f, r + 1]], axis=1)


class Sems:
    def __init__(self, send, recv):
        self.send, self.recv, self.n = send, recv, 0

    def take(self, count):
        at = self.n
        self.n += count
        return list(range(at, at + count))


N_SEMS = 192
N_LOCAL = 32


def when(cond, fn):
    if cond is None:
        fn()
    else:
        pl.when(cond)(fn)


def kernel(scale, sf, x_hbm, gain_in_hbm, win_hbm, gain_mid_hbm, wmid_hbm, wskip_hbm, sg_hbm,
           out_x, out_in, out_mid,
           OX, gain_in, gain_mid, wskip,
           XE, H1, SG, CE, CS, GE, GS, ACC, A1, H2, WIN, WMID, WTI, WTM,
           g_in, g_mid, rc_in, rc_mid, s_in, s_mid,
           a1_in, b1_in, a1_mid, b1_mid, p_in, p_mid, a2_in, b2_in, a2_mid, b2_mid,
           c_in, c_mid, z_in, z_mid, fin_in, fin_mid,
           send, recv, local):
    c = lax.axis_index("dp")
    t = lax.axis_index("tm")
    h = lax.axis_index("height")
    y, x_lo = t % 4, t // 4
    z, x_hi = h // 2, h % 2
    xx = x_hi * 2 + x_lo
    sems = Sems(send, recv)
    sent = []

    def dev(tt=None, hh=None, cc=None):
        d = {}
        d["dp"] = c if cc is None else cc
        d["tm"] = t if tt is None else tt
        d["height"] = h if hh is None else hh
        return d

    def x_peer(v):
        return dev(tt=y + 4 * (v % 2), hh=z * 2 + v // 2)

    def y_peer(v):
        return dev(tt=x_lo * 4 + v)

    def z_peer(v):
        return dev(hh=v * 2 + x_hi)

    kept = []

    def keep(src, dst):
        copy = pltpu.make_async_copy(src, dst, local.at[7 + len(kept)])
        copy.start()
        kept.append(copy)

    class Copy:
        def __init__(self, src, dst, to, s_if=None, r_if=None):
            i = sems.take(1)[0]
            self.d = pltpu.make_async_remote_copy(
                src_ref=src, dst_ref=dst, send_sem=send.at[i], recv_sem=recv.at[i],
                device_id=to, device_id_type=MESH)
            self.s_if, self.r_if = s_if, r_if

        def start(self):
            when(self.s_if, lambda: self.d.start())
            sent.append(self)

        def got(self):
            when(self.r_if, lambda: self.d.wait_recv())

        def left(self):
            when(self.s_if, lambda: self.d.wait_send())

    loc = [
        pltpu.make_async_copy(x_hbm.at[0], XE.at[pl.ds(2, FR), pl.ds(1, RW)], local.at[0]),
        pltpu.make_async_copy(sg_hbm.at[0], SG.at[pl.ds(SC * t, SC)], local.at[1]),
        pltpu.make_async_copy(win_hbm, WIN, local.at[2]),
        pltpu.make_async_copy(wmid_hbm, WMID, local.at[3]),
        pltpu.make_async_copy(gain_in_hbm, gain_in, local.at[4]),
        pltpu.make_async_copy(gain_mid_hbm, gain_mid, local.at[5]),
        pltpu.make_async_copy(wskip_hbm, wskip, local.at[6]),
    ]
    for item in loc:
        item.start()

    barrier = pltpu.get_barrier_semaphore()
    friends = [dev(hh=(h + k) % HT) for k in (8, 6, 10, 4, 12, 2, 14, 1, 15)]
    friends += [dev(tt=(t + a) % TM, hh=(h + b) % HT) for a in (1, 7) for b in (1, 15)]
    friends += [y_peer((y + k) % 4) for k in (1, 2, 3)]
    friends += [dev(tt=(t + k) % TM) for k in (1, 7, 4)]
    friends += [x_peer(3 - xx), dev(cc=1 - c)]
    for to in friends:
        pl.semaphore_signal(barrier, inc=1, device_id=to, device_id_type=MESH)

    first_t, last_t, first_h, last_h = t == 0, t == TM - 1, h == 0, h == HT - 1

    def zero(ref, f0, nf, r0, nr, ch):
        def body():
            for f in range(f0, f0 + nf):
                for r in range(r0, r0 + nr):
                    ref[f, r] = jnp.zeros((ch, W), BF16)
        return body

    pl.when(first_t)(zero(XE, 0, 2, 0, 4, CI))
    pl.when(jnp.logical_and(first_h, t > 0))(zero(XE, 0, 2, 0, 1, CI))
    pl.when(jnp.logical_and(last_h, t > 0))(zero(XE, 0, 2, 3, 1, CI))
    pl.when(first_h)(zero(XE, 2, 4, 0, 1, CI))
    pl.when(last_h)(zero(XE, 2, 4, 3, 1, CI))
    pl.when(first_h)(zero(CE, 0, 6, 0, 1, CO))
    pl.when(last_h)(zero(CE, 0, 6, 3, 1, CO))
    pl.when(last_t)(zero(GE, 4, 2, 0, 4, CO))
    pl.when(jnp.logical_and(first_h, t < TM - 1))(zero(GE, 4, 2, 0, 1, CO))
    pl.when(jnp.logical_and(last_h, t < TM - 1))(zero(GE, 4, 2, 3, 1, CO))
    pl.when(first_h)(zero(GE, 0, 4, 0, 1, CO))
    pl.when(last_h)(zero(GE, 0, 4, 3, 1, CO))

    pl.semaphore_wait(barrier, len(friends))

    both = jnp.logical_and
    has_n, has_p = h < HT - 1, h > 0
    t_n, t_p = t < TM - 1, t > 0

    other_t = (t + TM // 2) % TM
    across = [Copy(sg_hbm.at[0, j], SG.at[SC * t + j], dev(tt=other_t)) for j in range(SC)]
    along = [Copy(sg_hbm.at[0], SG.at[pl.ds(SC * t, SC)], y_peer((y + k) % 4)) for k in (1, 3, 2)]
    for item in across + along:
        item.start()

    src = x_hbm.at[0]
    x_halo = [
        Copy(src.at[:, 1], XE.at[pl.ds(2, 4), 0], dev(hh=h + 1), has_n, has_p),
        Copy(src.at[:, 0], XE.at[pl.ds(2, 4), 3], dev(hh=h - 1), has_p, has_n),
        Copy(src.at[pl.ds(2, 2)], XE.at[pl.ds(0, 2), pl.ds(1, 2)], dev(tt=t + 1), t_n, t_p),
        Copy(src.at[pl.ds(2, 2), 1], XE.at[pl.ds(0, 2), 0], dev(tt=t + 1, hh=h + 1),
             both(t_n, has_n), both(t_p, has_p)),
        Copy(src.at[pl.ds(2, 2), 0], XE.at[pl.ds(0, 2), 3], dev(tt=t + 1, hh=h - 1),
             both(t_n, has_p), both(t_p, has_n)),
    ]
    for item in x_halo[:2]:
        item.start()

    for j in range(SC):
        across[j].got()
        at_j = SC * other_t + j
        onward = [Copy(SG.at[at_j], SG.at[at_j], y_peer((y + k) % 4)) for k in (1, 3, 2)]
        for item in onward:
            item.start()
        along += onward
    for item in x_halo[2:]:
        item.start()

    for item in loc[4:]:
        item.wait()
    g1 = column(gain_in[...], CI)
    g2 = column(gain_mid[...], CO)

    def h1_at(f, r):
        H1[f, r] = norm_fwd(XE[f, r].astype(F32), g1).astype(BF16)

    loc[2].wait()
    loc[3].wait()

    def turn(i, _):
        kt, kh, kw = i // 9, (i // 3) % 3, i % 3
        WTI[i] = WIN[kt, kh, kw].astype(F32).T.astype(BF16)
        WTM[i] = WMID[kt, kh, kw].astype(F32).T.astype(BF16)
        return 0

    lax.fori_loop(0, 27, turn, 0)
    loc[0].wait()

    def h1_own(i, _):
        h1_at(2 + i // 2, 1 + i % 2)
        return 0

    lax.fori_loop(0, 8, h1_own, 0)

    loc[1].wait()
    for item in along:
        item.got()
    for f in range(6):
        frame = t * FR + f
        at = jnp.int32(0)
        found = jnp.int32(0)
        for j in range(SC * TM):
            hit = (sf[0, j] == frame).astype(jnp.int32)
            at = jnp.maximum(at, j * hit)
            found = jnp.maximum(found, hit)
        factor = found.astype(F32)
        for r in range(RW):
            CE[f, 1 + r] = (SG[at, r].astype(F32) * factor).astype(BF16)
    cot_halo = [
        Copy(CE.at[:, 2], CE.at[:, 0], dev(hh=h + 1), has_n, has_p),
        Copy(CE.at[:, 1], CE.at[:, 3], dev(hh=h - 1), has_p, has_n),
    ]
    for item in cot_halo:
        item.start()

    skip_a = jnp.zeros((CO, W), F32)
    skip_b = jnp.zeros((CO, W), F32)
    for f in range(FR):
        cot = pair(CE, f, 1)
        xs = pair(XE, 2 + f, 1)
        skip_a = skip_a + dot_nt(cot, xs[:W])
        skip_b = skip_b + dot_nt(cot, jnp.concatenate([jnp.zeros((64, 2 * W), BF16), xs[W:]], axis=0))
    g_mid[pl.ds(2016, 32)] = skip_a[:32].astype(BF16)
    g_in[pl.ds(2016, 32)] = skip_a[32:64].astype(BF16)
    g_in[pl.ds(4064, 32)] = skip_a[64:].astype(BF16)

    def mid_part(g, r, khs):
        acc = jnp.zeros((3 * CO, 2 * W), F32)
        for kt in range(3):
            for kh in khs:
                f, row = 2 * g + 2 - kt, r + 2 - kh
                matrix = WTM[pl.ds(9 * kt + 3 * kh, 3)].reshape(3 * CO, CO)
                acc = acc + dot(matrix, jnp.concatenate([CE[f, row], CE[f + 1, row]], axis=1))
        return acc

    def own_mid(g, _):
        ACC[g, 0] = mid_part(g, 0, (0, 1))
        ACC[g, 1] = mid_part(g, 1, (1, 2))
        return 0

    lax.fori_loop(0, 2, own_mid, 0)

    for item in x_halo[:2]:
        item.got()

    def h1_rows(f, _):
        h1_at(f, 0)
        h1_at(f, 3)
        return 0

    def h1_prior(f, _):
        h1_at(f, 1)
        h1_at(f, 2)
        return 0

    def forward(f, _):
        acc = jnp.zeros((3 * CO, 2 * W), F32)
        for kt, kh in TAPS:
            acc = acc + dot(WIN[kt, kh].reshape(3 * CO, CI), pair(H1, f + kt, kh))
        for r in range(RW):
            part = acc[:, r * W:(r + 1) * W]
            a1 = part[CO:2 * CO] + behind(part[:CO]) + ahead(part[2 * CO:])
            a1 = a1.astype(BF16)
            A1[f, r] = a1
            H2[f, r] = norm_fwd(a1.astype(F32), g2).astype(BF16)
        return 0

    lax.fori_loop(2, 6, h1_rows, 0)
    lax.fori_loop(2, FR, forward, 0)
    x_halo[2].got()
    lax.fori_loop(0, 2, h1_prior, 0)
    for item in x_halo[3:]:
        item.got()
    lax.fori_loop(0, 2, h1_rows, 0)
    lax.fori_loop(0, 2, forward, 0)

    for item in cot_halo:
        item.got()

    def back_mid(g, _):
        for r in range(RW):
            acc = ACC[g, r] + mid_part(g, r, (2,) if r == 0 else (0,))
            for j in range(2):
                f = 2 * g + j
                part = acc[:, j * W:(j + 1) * W]
                gh2 = part[CO:2 * CO] + ahead(part[:CO]) + behind(part[2 * CO:])
                ga1 = norm_pull(A1[f, r].astype(F32), g2, gh2).astype(BF16)
                GE[f, 1 + r] = ga1
                wide = ga1.astype(F32)
                lanes = pl.ds(r * W, W)
                GS[f, pl.ds(0, CO), lanes] = ahead(wide).astype(BF16)
                GS[f, pl.ds(CO, CO), lanes] = ga1
                GS[f, pl.ds(2 * CO, CO), lanes] = behind(wide).astype(BF16)
        return 0

    lax.fori_loop(0, 2, back_mid, 0)
    ga_halo = [
        Copy(GE.at[pl.ds(0, 4), 2], GE.at[pl.ds(0, 4), 0], dev(hh=h + 1), has_n, has_p),
        Copy(GE.at[pl.ds(0, 4), 1], GE.at[pl.ds(0, 4), 3], dev(hh=h - 1), has_p, has_n),
        Copy(GE.at[pl.ds(0, 2), pl.ds(1, 2)], GE.at[pl.ds(4, 2), pl.ds(1, 2)], dev(tt=t - 1), t_p, t_n),
        Copy(GE.at[pl.ds(0, 2), 2], GE.at[pl.ds(4, 2), 0], dev(tt=t - 1, hh=h + 1),
             both(t_p, has_n), both(t_n, has_p)),
        Copy(GE.at[pl.ds(0, 2), 1], GE.at[pl.ds(4, 2), 3], dev(tt=t - 1, hh=h - 1),
             both(t_p, has_p), both(t_n, has_n)),
    ]
    for item in ga_halo:
        item.start()

    def reduce(g, rc, s, a1, b1, p, a2, b2, cc, zz, fin, out, rows, parts=None):
        half = rows // 2
        ha = half // 2
        q = ha // 4
        e = q // 4
        owners = 2 * e // 16
        mine = pl.multiple_of(c * half, half)
        other = pl.multiple_of((1 - c) * half, half)

        def at(off, n):
            return pl.ds(pl.multiple_of(off, 16), n)

        def total(terms):
            out = terms[0].astype(F32)
            for term in terms[1:]:
                out = out + term.astype(F32)
            return out.astype(BF16)

        near = (1, 3, 2)
        far = (2, 1, 3, 0)

        def piece_a(base, k):
            return at(base + (xx + 4 - k) % 4 * q, q)

        def piece_b(base, k):
            return at(base + ha + (y + 4 - k) % 4 * q, q)

        core = []
        if parts:
            for off, n in parts:
                core.append(Copy(g.at[at(other + off, n)], rc.at[pl.ds(off, n)], dev(cc=1 - c)))
                core[-1].start()
                yield
            for item in core:
                item.got()
            core = []
        else:
            for k in far:
                for piece in (piece_a, piece_b):
                    core.append(Copy(g.at[piece(other, k)], rc.at[piece(0, k)], dev(cc=1 - c)))
                    core[-1].start()
            yield
        one = []
        for k in far[:3]:
            for n, piece in enumerate((piece_a, piece_b)):
                if core:
                    core.pop(0).got()
                s[piece(0, k)] = total([g[piece(mine, k)], rc[piece(0, k)]])
                if n == 0:
                    one.append(Copy(s.at[piece(0, k)], a1.at[k - 1], x_peer((xx + 4 - k) % 4)))
                else:
                    one.append(Copy(s.at[piece(0, k)], b1.at[k - 1], y_peer((y + 4 - k) % 4)))
                one[-1].start()
        for item in core:
            item.got()
        yield
        for item in one:
            item.got()
        p[pl.ds(0, q)] = total([g[piece_a(mine, 0)], rc[piece_a(0, 0)], a1[0], a1[1], a1[2]])
        p[pl.ds(q, q)] = total([g[piece_b(mine, 0)], rc[piece_b(0, 0)], b1[0], b1[1], b1[2]])
        two = []
        for k in (2, 1, 3):
            xp, yp = (xx + k) % 4, (y + k) % 4
            two.append(Copy(p.at[at(yp * e, e)], a2.at[k - 1], y_peer(yp)))
            two.append(Copy(p.at[at(q + xp * e, e)], b2.at[k - 1], x_peer(xp)))
        for item in two:
            item.start()
        yield
        for item in two:
            item.got()
        cc[pl.ds(0, e)] = total([p[at(y * e, e)], a2[0], a2[1], a2[2]])
        cc[pl.ds(e, e)] = total([p[at(q + xx * e, e)], b2[0], b2[1], b2[2]])
        ks = (4, 3, 5, 2, 6, 1, 7)
        own = None if owners == 8 else z < owners
        three = []
        for k in ks:
            zp = (z + k) % 8
            three.append(Copy(cc.at[at(zp % owners * 16, 16)], zz.at[k - 1], z_peer(zp),
                              None if owners == 8 else zp < owners, own))
        for item in three:
            item.start()
        yield
        for item in three:
            item.got()
        chain_b = (z >= owners // 2).astype(jnp.int32)
        zt = z % (owners // 2)
        base_a = mine + xx * q + y * e
        base_b = mine + ha + y * q + xx * e
        place = base_a + chain_b * (base_b - base_a) + zt * 16

        def finish():
            fin[at(place, 16)] = total([cc[at(z % owners * 16, 16)]] + [zz[k] for k in range(7)])

        when(own, finish)
        four = []
        for k in ks:
            zp, zm = (z + k) % 8, (z + 8 - k) % 8
            four.append(Copy(fin.at[at(place, 16)], fin.at[at(place, 16)], z_peer(zp),
                             own, None if owners == 8 else zm < owners))
        for item in four:
            item.start()
        yield
        for item in four:
            item.got()
        def part_a(k):
            return at(mine + xx * q + (y + 4 - k) % 4 * e, e)

        def part_b(k):
            return at(mine + ha + y * q + (xx + 4 - k) % 4 * e, e)

        six = {k: [] for k in near}

        def onward(k):
            for m in (2, 1, 3):
                six[m].append((Copy(fin.at[part_a(k)], fin.at[part_a(k)], x_peer((xx + m) % 4)),
                               Copy(fin.at[part_b(k)], fin.at[part_b(k)], y_peer((y + m) % 4))))
                for item in six[m][-1]:
                    item.start()

        five = {}
        for k in (2, 1, 3):
            five[k] = (Copy(fin.at[part_a(0)], fin.at[part_a(0)], y_peer((y + k) % 4)),
                       Copy(fin.at[part_b(0)], fin.at[part_b(0)], x_peer((xx + k) % 4)))
            for item in five[k]:
                item.start()
        onward(0)
        yield
        for k in near:
            for item in five[k]:
                item.got()
            onward(k)
        last = []

        def deliver(k):
            for piece in (piece_a, piece_b):
                rng = piece(mine, k)
                last.append(Copy(fin.at[rng], out.at[rng], dev(cc=1 - c)))
                last[-1].start()
                keep(fin.at[rng], out.at[rng])

        deliver(0)
        yield
        for m in near:
            for items in six[m]:
                for item in items:
                    item.got()
            deliver(m)
        yield
        for item in last:
            item.got()
        yield

    big = reduce(g_in, rc_in, s_in, a1_in, b1_in, p_in, a2_in, b2_in, c_in, z_in, fin_in, out_in, ROWS_IN,
                 [(432 * n, 432) for n in range(4)] + [(1728, 320)])
    small = reduce(g_mid, rc_mid, s_mid, a1_mid, b1_mid, p_mid, a2_mid, b2_mid, c_mid, z_mid, fin_mid, out_mid, ROWS_MID)
    for n, taps in enumerate(PAIRS):
        acc = jnp.zeros((3 * CO, 3 * W), F32)
        for f in range(FR):
            one = [pair(H1, f + TAPS[i][0], TAPS[i][1]) for i in taps]
            rhs = jnp.concatenate([one[0][:W], one[1][:W], one[0][W:], one[1][W:]], axis=0)
            acc = acc + dot_nt(GS[f], rhs)
        blocks = [acc[:, j * W:(j + 1) * W].astype(BF16) for j in range(3)]
        g_in[pl.ds(432 * n, 288)] = blocks[0]
        g_in[pl.ds(432 * n + 288, 144)] = blocks[1][:144]
        g_in[pl.ds(2048 + 432 * n, 144)] = blocks[1][144:]
        g_in[pl.ds(2048 + 432 * n + 144, 288)] = blocks[2]
        next(big)
    acc = jnp.zeros((3 * CO, 2 * W), F32)
    for f in range(FR):
        rhs = jnp.concatenate([pair(H1, f + 2, 2), jnp.zeros((64, 2 * W), BF16)], axis=0)
        acc = acc + dot_nt(GS[f], rhs)
    for j in range(2):
        g_in[pl.ds(2048 * j + 1728, 288)] = acc[:, j * W:(j + 1) * W].astype(BF16)
    next(big)

    def cot_shift(f, _):
        for r in range(4):
            wide = CE[f, r].astype(F32)
            lanes = pl.ds(r * W, W)
            CS[f, pl.ds(0, CO), lanes] = ahead(wide).astype(BF16)
            CS[f, pl.ds(CO, CO), lanes] = CE[f, r]
            CS[f, pl.ds(2 * CO, CO), lanes] = behind(wide).astype(BF16)
        return 0

    lax.fori_loop(0, 6, cot_shift, 0)

    def cot_window(f, tap):
        kt, kh = TAPS[tap]
        return CS[f + 2 - kt, :, pl.ds((2 - kh) * W, 2 * W)]

    for n in range(2):
        acc = jnp.zeros((CO, 9 * W), F32)
        for f in range(FR):
            rhs = jnp.concatenate([cot_window(f, 4 * n + i) for i in range(4)], axis=0)
            acc = acc + dot_nt(pair(H2, f, 0), rhs)
        for j in range(9):
            g_mid[pl.ds(864 * n + CO * j, CO)] = acc[:, j * W:(j + 1) * W].astype(BF16)
    acc = jnp.zeros((CO, 3 * W), F32)
    for f in range(FR):
        rhs = jnp.concatenate([cot_window(f, 8), jnp.zeros((CO, 2 * W), BF16)], axis=0)
        acc = acc + dot_nt(pair(H2, f, 0), rhs)
    g_mid[pl.ds(1728, CO)] = acc[:, :W].astype(BF16)
    g_mid[pl.ds(1824, CO)] = acc[:, W:2 * W].astype(BF16)
    g_mid[pl.ds(1920, CO)] = (acc[:, 2 * W:] + skip_b).astype(BF16)

    next(small)
    next(big)
    next(small)

    def back_in(f):
        acc = jnp.zeros((3 * CI, 2 * W), F32)
        for n, (kt, kh) in enumerate(TAPS):
            acc = acc + dot(WTI[pl.ds(3 * n, 3)].reshape(3 * CI, CO), pair(GE, f + 2 - kt, 2 - kh))
        skip = lax.dot_general(wskip[...], pair(CE, f, 1), (((0,), (0,)), ((), ())),
                               preferred_element_type=F32)
        for r in range(RW):
            part = acc[:, r * W:(r + 1) * W]
            gh1 = part[CI:2 * CI] + ahead(part[:CI]) + behind(part[2 * CI:])
            grad = norm_pull(XE[2 + f, 1 + r].astype(F32), g1, gh1) + skip[:, r * W:(r + 1) * W]
            OX[f, r] = grad.astype(BF16)

    for item in ga_halo:
        item.got()
    for f in range(FR):
        back_in(f)
        next(big)
        next(small)
    keep(OX, out_x.at[0])
    for _ in range(3):
        next(big)
        next(small)
    for item in sent:
        item.left()
    for item in kept:
        item.wait()


def assemble(scale, gx_hbm, fi_hbm, fm_hbm, out_x, out_in, out_mid, out_skip, gx, fi, fm, BI, BM, BS, sem, got):
    copies = []

    def put(src, dst):
        copy = pltpu.make_async_copy(src, dst, sem.at[len(copies)])
        copy.start()
        copies.append(copy)

    def load(src, dst, i):
        copy = pltpu.make_async_copy(src, dst, got.at[i])
        copy.start()
        return copy

    need_in = []
    for n in range(5):
        count = 432 if n < 4 else 320
        need_in.append([load(fi_hbm.at[pl.ds(at, count)], fi.at[pl.ds(at, count)], 2 * n + k)
                        for k, at in enumerate((432 * n, 2048 + 432 * n))])
    need_mid = []
    for n in range(5):
        part = pl.ds(480 * n, 480 if n < 4 else 128)
        need_mid.append(load(fm_hbm.at[part], fm.at[part], 10 + n))
    need_x = load(gx_hbm, gx, 15)

    def rows(n, at, count):
        if at + count <= 432:
            value = fi[pl.ds(432 * n + at, count)]
        elif at >= 432:
            value = fi[pl.ds(2048 + 432 * n + at - 432, count)]
        else:
            cut = 432 - at
            value = jnp.concatenate([fi[pl.ds(432 * n + at, cut)], fi[pl.ds(2048 + 432 * n, count - cut)]], axis=0)
        return value.astype(F32) * scale

    for n, taps in enumerate(PAIRS):
        for item in need_in[n]:
            item.wait()
        for kw in range(3):
            low = rows(n, 576 + CO * kw, CO)
            for j, i in enumerate(taps):
                kt, kh = TAPS[i]
                BI[kt, kh, kw, :, pl.ds(0, W)] = rows(n, 288 * j + CO * kw, CO)
                rest = low if j == 0 else pltpu.roll(low, 64, 1)
                BI[kt, kh, kw, :, pl.ds(W, 64)] = rest[:, :64]
        for i in taps:
            put(BI.at[TAPS[i]], out_in.at[TAPS[i]])
    for item in need_in[4]:
        item.wait()
    for kw in range(3):
        BI[2, 2, kw, :, pl.ds(0, W)] = fi[pl.ds(1728 + CO * kw, CO)].astype(F32) * scale
        BI[2, 2, kw, :, pl.ds(W, 64)] = (fi[pl.ds(3776 + CO * kw, CO)].astype(F32) * scale)[:, :64]
    put(BI.at[2, 2], out_in.at[2, 2])
    need_x.wait()
    put(gx, out_x)
    need_mid[4].wait()
    tail = fm[pl.ds(1920, CO)].astype(F32) * scale
    BS[pl.ds(0, 32), pl.ds(0, W)] = fm[pl.ds(2016, 32)].astype(F32) * scale
    BS[pl.ds(32, 32), pl.ds(0, W)] = fi[pl.ds(2016, 32)].astype(F32) * scale
    BS[pl.ds(64, 32), pl.ds(0, W)] = fi[pl.ds(4064, 32)].astype(F32) * scale
    BS[:, pl.ds(W, 64)] = pltpu.roll(tail, 64, 1)[:, :64]
    put(BS, out_skip)
    for j in range(20):
        if j % 5 == 0:
            need_mid[j // 5].wait()
        BM[pl.ds(W * j, W)] = (fm[pl.ds(CO * j, CO)].astype(F32) * scale).T
        if j % 5 == 4:
            rows = pl.ds(W * (j - 4), 5 * W)
            put(BM.at[rows], out_mid.at[rows])
    BM[pl.ds(2560, 32)] = tail.T[:32]
    put(BM.at[pl.ds(2560, 32)], out_mid.at[pl.ds(2560, 32)])
    for copy in copies:
        copy.wait()


def reduce_scratch(rows):
    half = rows // 2
    q, e = half // 8, half // 32
    return {
        "g": (rows, W), "rc": (half, W), "s": (half, W), "a1": (3, q, W), "b1": (3, q, W), "p": (2 * q, W),
        "a2": (3, e, W), "b2": (3, e, W), "c": (2 * e, W), "z": (7, 16, W), "fin": (rows, W),
    }


def shards(inputs, gain_in, conv_in, gain_mid, conv_mid, conv_skip, scored_grads, scored_frames):
    count = scored_frames.shape[1] * inputs.shape[0] * lax.axis_size("dp")
    scale = 1.0 / math.sqrt(count * RW * HT * W)
    anyw = pl.BlockSpec(memory_space=pl.ANY)
    smem = pl.BlockSpec(memory_space=pltpu.SMEM)
    big, small = reduce_scratch(ROWS_IN), reduce_scratch(ROWS_MID)

    def buf(shape, dtype=BF16):
        return pltpu.VMEM(shape, dtype)

    scratch = [
        buf((FR, RW, CI, W)), buf((1, CI), F32), buf((1, CO), F32), buf((CO, CI)),
        buf((6, 4, CI, W)), buf((6, 4, CI, W)), buf((SC * TM, RW, CO, W)), buf((6, 4, CO, W)),
        buf((6, 3 * CO, 4 * W)), buf((6, 4, CO, W)), buf((FR, 3 * CO, RW * W)), buf((2, RW, 3 * CO, 2 * W), F32),
        buf((FR, RW, CO, W)), buf((FR, RW, CO, W)),
        buf((3, 3, 3, CO, CI)), buf((3, 3, 3, CO, CO)), buf((27, CI, CO)), buf((27, CO, CO)),
    ]
    for name in ("g", "rc", "s"):
        scratch += [buf(big[name]), buf(small[name])]
    scratch += [buf(big["a1"]), buf(big["b1"]), buf(small["a1"]), buf(small["b1"])]
    scratch += [buf(big["p"]), buf(small["p"])]
    scratch += [buf(big["a2"]), buf(big["b2"]), buf(small["a2"]), buf(small["b2"])]
    for name in ("c", "z", "fin"):
        scratch += [buf(big[name]), buf(small[name])]
    scratch += [
        pltpu.SemaphoreType.DMA((N_SEMS,)), pltpu.SemaphoreType.DMA((N_SEMS,)),
        pltpu.SemaphoreType.DMA((N_LOCAL,)),
    ]

    def body(*refs):
        kernel(scale, *refs)

    grad_x, sum_in, sum_mid = pl.pallas_call(
        body,
        out_shape=(
            jax.ShapeDtypeStruct(inputs.shape, BF16),
            jax.ShapeDtypeStruct((ROWS_IN, W), BF16),
            jax.ShapeDtypeStruct((ROWS_MID, W), BF16),
        ),
        in_specs=[smem] + [anyw] * 7,
        out_specs=(anyw, anyw, anyw),
        scratch_shapes=scratch,
        compiler_params=pltpu.CompilerParams(
            collective_id=0, has_side_effects=True, vmem_limit_bytes=63 * 1024 * 1024
        ),
        name="block_backward",
    )(scored_frames, inputs, gain_in[None, :], conv_in, gain_mid[None, :], conv_mid, conv_skip, scored_grads)

    def last(*refs):
        assemble(scale, *refs)

    grad_inputs, grad_in, grad_mid, grad_skip = pl.pallas_call(
        last,
        out_shape=(
            jax.ShapeDtypeStruct(inputs.shape, BF16),
            jax.ShapeDtypeStruct(conv_in.shape, F32),
            jax.ShapeDtypeStruct((27 * CO, CO), F32),
            jax.ShapeDtypeStruct(conv_skip.shape, F32),
        ),
        in_specs=[anyw, anyw, anyw],
        out_specs=(anyw, anyw, anyw, anyw),
        scratch_shapes=[
            buf(inputs.shape), buf((ROWS_IN, W)), buf((ROWS_MID, W)),
            buf(conv_in.shape, F32), buf((27 * CO, CO), F32), buf(conv_skip.shape, F32),
            pltpu.SemaphoreType.DMA((16,)), pltpu.SemaphoreType.DMA((16,)),
        ],
        compiler_params=pltpu.CompilerParams(vmem_limit_bytes=63 * 1024 * 1024),
        name="assemble",
    )(grad_x, sum_in, sum_mid)
    return grad_inputs, grad_in, grad_mid.reshape(conv_mid.shape), grad_skip


def solution(mesh):
    in_specs = (
        P("dp", "tm", "height", None, None),
        P(),
        P(),
        P(),
        P(),
        P(),
        P("dp", "tm", "height", None, None),
        P("dp", None),
    )
    out_specs = (P("dp", "tm", "height", None, None), P(), P(), P())
    return jax.shard_map(shards, mesh=mesh, in_specs=in_specs, out_specs=out_specs, check_vma=False)
```

```python
import math

import jax
import jax.numpy as jnp
from jax import lax
from jax.experimental import pallas as pl
from jax.experimental.pallas import tpu as pltpu
from jax.sharding import PartitionSpec as P

MESH = pl.DeviceIdType.MESH
F32 = jnp.float32
BF16 = jnp.bfloat16
FR, RW, CI, CO, W = 4, 2, 192, 96, 128
TM, HT = 8, 16
SC = 2
EPS = 1e-06
TAPS = [(kt, kh) for kt in range(3) for kh in range(3)]
PAIRS = [(0, 1), (2, 3), (4, 5), (6, 7)]
ROWS_IN, ROWS_MID = 4096, 2048


def sigmoid(u):
    return 1.0 / (1.0 + jnp.exp(-u))


def norm_parts(v, g):
    s = lax.rsqrt(jnp.mean(v * v, axis=0, keepdims=True) + EPS)
    n = v * s
    u = n * g
    return s, n, u, sigmoid(u)


def norm_fwd(v, g):
    _, _, u, sg = norm_parts(v, g)
    return u * sg


def norm_pull(v, g, ct):
    s, n, u, sg = norm_parts(v, g)
    dn = ct * (sg * (1.0 + u * (1.0 - sg))) * g
    return s * (dn - n * jnp.mean(dn * n, axis=0, keepdims=True))


def ahead(v):
    lane = lax.broadcasted_iota(jnp.int32, v.shape, 1)
    return jnp.where(lane == W - 1, 0.0, pltpu.roll(v, W - 1, 1))


def behind(v):
    lane = lax.broadcasted_iota(jnp.int32, v.shape, 1)
    return jnp.where(lane == 0, 0.0, pltpu.roll(v, 1, 1))


def column(row, n):
    r = lax.broadcasted_iota(jnp.int32, (n, n), 0)
    c = lax.broadcasted_iota(jnp.int32, (n, n), 1)
    return jnp.sum(jnp.where(r == c, jnp.broadcast_to(row, (n, n)), 0.0), axis=1, keepdims=True)


def dot(a, b):
    return jnp.dot(a, b, preferred_element_type=F32)


def dot_nt(a, b):
    return lax.dot_general(a, b, (((1,), (1,)), ((), ())), preferred_element_type=F32)


def pair(ref, f, r):
    return jnp.concatenate([ref[f, r], ref[f, r + 1]], axis=1)


class Sems:
    def __init__(self, send, recv):
        self.send, self.recv, self.n = send, recv, 0

    def take(self, count):
        at = self.n
        self.n += count
        return list(range(at, at + count))


N_SEMS = 192
N_LOCAL = 32


def when(cond, fn):
    if cond is None:
        fn()
    else:
        pl.when(cond)(fn)


def kernel(scale, sf, x_hbm, gain_in_hbm, win_hbm, gain_mid_hbm, wmid_hbm, wskip_hbm, sg_hbm,
           out_x, out_in, out_mid,
           OX, gain_in, gain_mid, wskip,
           XE, H1, SG, CE, CS, GE, GS, ACC, A1, H2, WIN, WMID, WTI, WTM,
           g_in, g_mid, rc_in, rc_mid, s_in, s_mid,
           a1_in, b1_in, a1_mid, b1_mid, p_in, p_mid, a2_in, b2_in, a2_mid, b2_mid,
           c_in, c_mid, z_in, z_mid, fin_in, fin_mid,
           send, recv, local):
    c = lax.axis_index("dp")
    t = lax.axis_index("tm")
    h = lax.axis_index("height")
    y, x_lo = t % 4, t // 4
    z, x_hi = h // 2, h % 2
    xx = x_hi * 2 + x_lo
    sems = Sems(send, recv)
    sent = []

    def dev(tt=None, hh=None, cc=None):
        d = {}
        d["dp"] = c if cc is None else cc
        d["tm"] = t if tt is None else tt
        d["height"] = h if hh is None else hh
        return d

    def x_peer(v):
        return dev(tt=y + 4 * (v % 2), hh=z * 2 + v // 2)

    def y_peer(v):
        return dev(tt=x_lo * 4 + v)

    def z_peer(v):
        return dev(hh=v * 2 + x_hi)

    kept = []

    def keep(src, dst):
        copy = pltpu.make_async_copy(src, dst, local.at[7 + len(kept)])
        copy.start()
        kept.append(copy)

    class Copy:
        def __init__(self, src, dst, to, s_if=None, r_if=None):
            i = sems.take(1)[0]
            self.d = pltpu.make_async_remote_copy(
                src_ref=src, dst_ref=dst, send_sem=send.at[i], recv_sem=recv.at[i],
                device_id=to, device_id_type=MESH)
            self.s_if, self.r_if = s_if, r_if

        def start(self):
            when(self.s_if, lambda: self.d.start())
            sent.append(self)

        def got(self):
            when(self.r_if, lambda: self.d.wait_recv())

        def left(self):
            when(self.s_if, lambda: self.d.wait_send())

    loc = [
        pltpu.make_async_copy(x_hbm.at[0], XE.at[pl.ds(2, FR), pl.ds(1, RW)], local.at[0]),
        pltpu.make_async_copy(sg_hbm.at[0], SG.at[pl.ds(SC * t, SC)], local.at[1]),
        pltpu.make_async_copy(win_hbm, WIN, local.at[2]),
        pltpu.make_async_copy(wmid_hbm, WMID, local.at[3]),
        pltpu.make_async_copy(gain_in_hbm, gain_in, local.at[4]),
        pltpu.make_async_copy(gain_mid_hbm, gain_mid, local.at[5]),
        pltpu.make_async_copy(wskip_hbm, wskip, local.at[6]),
    ]
    for item in loc:
        item.start()

    barrier = pltpu.get_barrier_semaphore()
    friends = [dev(hh=(h + k) % HT) for k in (8, 6, 10, 4, 12, 2, 14, 1, 15)]
    friends += [dev(tt=(t + a) % TM, hh=(h + b) % HT) for a in (1, 7) for b in (1, 15)]
    friends += [y_peer((y + k) % 4) for k in (1, 2, 3)]
    friends += [dev(tt=(t + k) % TM) for k in (1, 7, 4)]
    friends += [x_peer(3 - xx), dev(cc=1 - c)]
    for to in friends:
        pl.semaphore_signal(barrier, inc=1, device_id=to, device_id_type=MESH)

    first_t, last_t, first_h, last_h = t == 0, t == TM - 1, h == 0, h == HT - 1

    def zero(ref, f0, nf, r0, nr, ch):
        def body():
            for f in range(f0, f0 + nf):
                for r in range(r0, r0 + nr):
                    ref[f, r] = jnp.zeros((ch, W), BF16)
        return body

    pl.when(first_t)(zero(XE, 0, 2, 0, 4, CI))
    pl.when(jnp.logical_and(first_h, t > 0))(zero(XE, 0, 2, 0, 1, CI))
    pl.when(jnp.logical_and(last_h, t > 0))(zero(XE, 0, 2, 3, 1, CI))
    pl.when(first_h)(zero(XE, 2, 4, 0, 1, CI))
    pl.when(last_h)(zero(XE, 2, 4, 3, 1, CI))
    pl.when(first_h)(zero(CE, 0, 6, 0, 1, CO))
    pl.when(last_h)(zero(CE, 0, 6, 3, 1, CO))
    pl.when(last_t)(zero(GE, 4, 2, 0, 4, CO))
    pl.when(jnp.logical_and(first_h, t < TM - 1))(zero(GE, 4, 2, 0, 1, CO))
    pl.when(jnp.logical_and(last_h, t < TM - 1))(zero(GE, 4, 2, 3, 1, CO))
    pl.when(first_h)(zero(GE, 0, 4, 0, 1, CO))
    pl.when(last_h)(zero(GE, 0, 4, 3, 1, CO))

    pl.semaphore_wait(barrier, len(friends))

    both = jnp.logical_and
    has_n, has_p = h < HT - 1, h > 0
    t_n, t_p = t < TM - 1, t > 0

    other_t = (t + TM // 2) % TM
    across = [Copy(sg_hbm.at[0, j], SG.at[SC * t + j], dev(tt=other_t)) for j in range(SC)]
    along = [Copy(sg_hbm.at[0], SG.at[pl.ds(SC * t, SC)], y_peer((y + k) % 4)) for k in (2, 1, 3)]
    for item in across + along:
        item.start()

    src = x_hbm.at[0]
    x_halo = [
        Copy(src.at[:, 1], XE.at[pl.ds(2, 4), 0], dev(hh=h + 1), has_n, has_p),
        Copy(src.at[:, 0], XE.at[pl.ds(2, 4), 3], dev(hh=h - 1), has_p, has_n),
        Copy(src.at[pl.ds(2, 2)], XE.at[pl.ds(0, 2), pl.ds(1, 2)], dev(tt=t + 1), t_n, t_p),
        Copy(src.at[pl.ds(2, 2), 1], XE.at[pl.ds(0, 2), 0], dev(tt=t + 1, hh=h + 1),
             both(t_n, has_n), both(t_p, has_p)),
        Copy(src.at[pl.ds(2, 2), 0], XE.at[pl.ds(0, 2), 3], dev(tt=t + 1, hh=h - 1),
             both(t_n, has_p), both(t_p, has_n)),
    ]
    for item in x_halo[:2]:
        item.start()

    for j in range(SC):
        across[j].got()
        at_j = SC * other_t + j
        onward = [Copy(SG.at[at_j], SG.at[at_j], y_peer((y + k) % 4)) for k in (2, 1, 3)]
        for item in onward:
            item.start()
        along += onward
    for item in x_halo[2:]:
        item.start()

    for item in loc[4:]:
        item.wait()
    g1 = column(gain_in[...], CI)
    g2 = column(gain_mid[...], CO)

    def h1_at(f, r):
        H1[f, r] = norm_fwd(XE[f, r].astype(F32), g1).astype(BF16)

    loc[2].wait()
    loc[3].wait()

    def turn(i, _):
        kt, kh, kw = i // 9, (i // 3) % 3, i % 3
        WTM[i] = WMID[kt, kh, kw].astype(F32).T.astype(BF16)
        return 0

    lax.fori_loop(0, 27, turn, 0)
    places = []
    for f in range(6):
        frame = t * FR + f
        at = jnp.int32(0)
        found = jnp.int32(0)
        for j in range(SC * TM):
            hit = (sf[0, j] == frame).astype(jnp.int32)
            at = jnp.maximum(at, j * hit)
            found = jnp.maximum(found, hit)
        places.append((at, found.astype(F32)))
    loc[1].wait()
    for item in along:
        item.got()
    for f, (at, factor) in enumerate(places):
        for r in range(RW):
            CE[f, 1 + r] = (SG[at, r].astype(F32) * factor).astype(BF16)
    cot_halo = [
        Copy(CE.at[:, 2], CE.at[:, 0], dev(hh=h + 1), has_n, has_p),
        Copy(CE.at[:, 1], CE.at[:, 3], dev(hh=h - 1), has_p, has_n),
    ]
    for item in cot_halo:
        item.start()

    loc[0].wait()

    def h1_own(i, _):
        h1_at(2 + i // 2, 1 + i % 2)
        return 0

    lax.fori_loop(0, 8, h1_own, 0)

    skip_a = jnp.zeros((CO, W), F32)
    skip_b = jnp.zeros((CO, W), F32)
    for f in range(FR):
        cot = pair(CE, f, 1)
        xs = pair(XE, 2 + f, 1)
        skip_a = skip_a + dot_nt(cot, xs[:W])
        skip_b = skip_b + dot_nt(cot, jnp.concatenate([jnp.zeros((64, 2 * W), BF16), xs[W:]], axis=0))
    g_mid[pl.ds(2016, 32)] = skip_a[:32].astype(BF16)
    g_in[pl.ds(2016, 32)] = skip_a[32:64].astype(BF16)
    g_in[pl.ds(4064, 32)] = skip_a[64:].astype(BF16)

    def mid_part(g, r, khs):
        acc = jnp.zeros((3 * CO, 2 * W), F32)
        for kt in range(3):
            for kh in khs:
                f, row = 2 * g + 2 - kt, r + 2 - kh
                matrix = WTM[pl.ds(9 * kt + 3 * kh, 3)].reshape(3 * CO, CO)
                acc = acc + dot(matrix, jnp.concatenate([CE[f, row], CE[f + 1, row]], axis=1))
        return acc

    def own_mid(g, _):
        ACC[g, 0] = mid_part(g, 0, (0, 1))
        ACC[g, 1] = mid_part(g, 1, (1, 2))
        return 0

    lax.fori_loop(0, 2, own_mid, 0)

    for item in x_halo[:2]:
        item.got()

    def h1_rows(f, _):
        h1_at(f, 0)
        h1_at(f, 3)
        return 0

    def h1_prior(f, _):
        h1_at(f, 1)
        h1_at(f, 2)
        return 0

    def forward(f, _):
        acc = jnp.zeros((3 * CO, 2 * W), F32)
        for kt, kh in TAPS:
            acc = acc + dot(WIN[kt, kh].reshape(3 * CO, CI), pair(H1, f + kt, kh))
        for r in range(RW):
            part = acc[:, r * W:(r + 1) * W]
            a1 = part[CO:2 * CO] + behind(part[:CO]) + ahead(part[2 * CO:])
            a1 = a1.astype(BF16)
            A1[f, r] = a1
            H2[f, r] = norm_fwd(a1.astype(F32), g2).astype(BF16)
        return 0

    lax.fori_loop(2, 6, h1_rows, 0)
    lax.fori_loop(2, FR, forward, 0)
    x_halo[2].got()
    lax.fori_loop(0, 2, h1_prior, 0)
    for item in x_halo[3:]:
        item.got()
    lax.fori_loop(0, 2, h1_rows, 0)
    lax.fori_loop(0, 2, forward, 0)

    for item in cot_halo:
        item.got()

    def back_mid(g, _):
        for r in range(RW):
            acc = ACC[g, r] + mid_part(g, r, (2,) if r == 0 else (0,))
            for j in range(2):
                f = 2 * g + j
                part = acc[:, j * W:(j + 1) * W]
                gh2 = part[CO:2 * CO] + ahead(part[:CO]) + behind(part[2 * CO:])
                ga1 = norm_pull(A1[f, r].astype(F32), g2, gh2).astype(BF16)
                GE[f, 1 + r] = ga1
                wide = ga1.astype(F32)
                lanes = pl.ds(r * W, W)
                GS[f, pl.ds(0, CO), lanes] = ahead(wide).astype(BF16)
                GS[f, pl.ds(CO, CO), lanes] = ga1
                GS[f, pl.ds(2 * CO, CO), lanes] = behind(wide).astype(BF16)
        return 0

    lax.fori_loop(0, 2, back_mid, 0)
    ga_halo = [
        Copy(GE.at[pl.ds(0, 4), 2], GE.at[pl.ds(0, 4), 0], dev(hh=h + 1), has_n, has_p),
        Copy(GE.at[pl.ds(0, 4), 1], GE.at[pl.ds(0, 4), 3], dev(hh=h - 1), has_p, has_n),
        Copy(GE.at[pl.ds(0, 2), pl.ds(1, 2)], GE.at[pl.ds(4, 2), pl.ds(1, 2)], dev(tt=t - 1), t_p, t_n),
        Copy(GE.at[pl.ds(0, 2), 2], GE.at[pl.ds(4, 2), 0], dev(tt=t - 1, hh=h + 1),
             both(t_p, has_n), both(t_n, has_p)),
        Copy(GE.at[pl.ds(0, 2), 1], GE.at[pl.ds(4, 2), 3], dev(tt=t - 1, hh=h - 1),
             both(t_p, has_p), both(t_n, has_n)),
    ]
    for item in ga_halo:
        item.start()

    def reduce(g, rc, s, a1, b1, p, a2, b2, cc, zz, fin, out, rows, parts=None):
        half = rows // 2
        ha = half // 2
        q = ha // 4
        e = q // 4
        owners = 2 * e // 16
        mine = pl.multiple_of(c * half, half)
        other = pl.multiple_of((1 - c) * half, half)

        def at(off, n):
            return pl.ds(pl.multiple_of(off, 16), n)

        def total(terms):
            out = terms[0].astype(F32)
            for term in terms[1:]:
                out = out + term.astype(F32)
            return out.astype(BF16)

        near = (1, 3, 2)
        far = (2, 1, 3, 0)

        def piece_a(base, k):
            return at(base + (xx + 4 - k) % 4 * q, q)

        def piece_b(base, k):
            return at(base + ha + (y + 4 - k) % 4 * q, q)

        core = []
        if parts:
            for off, n in parts:
                core.append(Copy(g.at[at(other + off, n)], rc.at[pl.ds(off, n)], dev(cc=1 - c)))
                core[-1].start()
                yield
            for item in core:
                item.got()
            core = []
        else:
            for k in far:
                for piece in (piece_a, piece_b):
                    core.append(Copy(g.at[piece(other, k)], rc.at[piece(0, k)], dev(cc=1 - c)))
                    core[-1].start()
            yield
        one = []
        for k in far[:3]:
            for n, piece in enumerate((piece_a, piece_b)):
                if core:
                    core.pop(0).got()
                s[piece(0, k)] = total([g[piece(mine, k)], rc[piece(0, k)]])
                if n == 0:
                    one.append(Copy(s.at[piece(0, k)], a1.at[k - 1], x_peer((xx + 4 - k) % 4)))
                else:
                    one.append(Copy(s.at[piece(0, k)], b1.at[k - 1], y_peer((y + 4 - k) % 4)))
                one[-1].start()
        for item in core:
            item.got()
        yield
        for item in one:
            item.got()
        p[pl.ds(0, q)] = total([g[piece_a(mine, 0)], rc[piece_a(0, 0)], a1[0], a1[1], a1[2]])
        p[pl.ds(q, q)] = total([g[piece_b(mine, 0)], rc[piece_b(0, 0)], b1[0], b1[1], b1[2]])
        two = []
        for k in (2, 1, 3):
            xp, yp = (xx + k) % 4, (y + k) % 4
            two.append(Copy(p.at[at(yp * e, e)], a2.at[k - 1], y_peer(yp)))
            two.append(Copy(p.at[at(q + xp * e, e)], b2.at[k - 1], x_peer(xp)))
        for item in two:
            item.start()
        yield
        for item in two:
            item.got()
        cc[pl.ds(0, e)] = total([p[at(y * e, e)], a2[0], a2[1], a2[2]])
        cc[pl.ds(e, e)] = total([p[at(q + xx * e, e)], b2[0], b2[1], b2[2]])
        ks = (4, 3, 5, 2, 6, 1, 7)
        own = None if owners == 8 else z < owners
        three = []
        for k in ks:
            zp = (z + k) % 8
            three.append(Copy(cc.at[at(zp % owners * 16, 16)], zz.at[k - 1], z_peer(zp),
                              None if owners == 8 else zp < owners, own))
        for item in three:
            item.start()
        yield
        for item in three:
            item.got()
        chain_b = (z >= owners // 2).astype(jnp.int32)
        zt = z % (owners // 2)
        base_a = mine + xx * q + y * e
        base_b = mine + ha + y * q + xx * e
        place = base_a + chain_b * (base_b - base_a) + zt * 16

        def finish():
            fin[at(place, 16)] = total([cc[at(z % owners * 16, 16)]] + [zz[k] for k in range(7)])

        when(own, finish)
        four = []
        for k in ks:
            zp, zm = (z + k) % 8, (z + 8 - k) % 8
            four.append(Copy(fin.at[at(place, 16)], fin.at[at(place, 16)], z_peer(zp),
                             own, None if owners == 8 else zm < owners))
        for item in four:
            item.start()
        yield
        for item in four:
            item.got()
        def part_a(k):
            return at(mine + xx * q + (y + 4 - k) % 4 * e, e)

        def part_b(k):
            return at(mine + ha + y * q + (xx + 4 - k) % 4 * e, e)

        six = {k: [] for k in near}

        def onward(k):
            for m in (2, 1, 3):
                six[m].append((Copy(fin.at[part_a(k)], fin.at[part_a(k)], x_peer((xx + m) % 4)),
                               Copy(fin.at[part_b(k)], fin.at[part_b(k)], y_peer((y + m) % 4))))
                for item in six[m][-1]:
                    item.start()

        five = {}
        for k in (2, 1, 3):
            five[k] = (Copy(fin.at[part_a(0)], fin.at[part_a(0)], y_peer((y + k) % 4)),
                       Copy(fin.at[part_b(0)], fin.at[part_b(0)], x_peer((xx + k) % 4)))
            for item in five[k]:
                item.start()
        onward(0)
        yield
        for k in near:
            for item in five[k]:
                item.got()
            onward(k)
        last = []

        def deliver(k):
            for piece in (piece_a, piece_b):
                rng = piece(mine, k)
                last.append(Copy(fin.at[rng], out.at[rng], dev(cc=1 - c)))
                last[-1].start()
                keep(fin.at[rng], out.at[rng])

        deliver(0)
        yield
        for m in near:
            for items in six[m]:
                for item in items:
                    item.got()
            deliver(m)
        yield
        for item in last:
            item.got()
        yield

    big = reduce(g_in, rc_in, s_in, a1_in, b1_in, p_in, a2_in, b2_in, c_in, z_in, fin_in, out_in, ROWS_IN,
                 [(432 * n, 432) for n in range(4)] + [(1728, 320)])
    small = reduce(g_mid, rc_mid, s_mid, a1_mid, b1_mid, p_mid, a2_mid, b2_mid, c_mid, z_mid, fin_mid, out_mid, ROWS_MID)
    for n, taps in enumerate(PAIRS):
        acc = jnp.zeros((3 * CO, 3 * W), F32)
        for f in range(FR):
            one = [pair(H1, f + TAPS[i][0], TAPS[i][1]) for i in taps]
            rhs = jnp.concatenate([one[0][:W], one[1][:W], one[0][W:], one[1][W:]], axis=0)
            acc = acc + dot_nt(GS[f], rhs)
        blocks = [acc[:, j * W:(j + 1) * W].astype(BF16) for j in range(3)]
        g_in[pl.ds(432 * n, 288)] = blocks[0]
        g_in[pl.ds(432 * n + 288, 144)] = blocks[1][:144]
        g_in[pl.ds(2048 + 432 * n, 144)] = blocks[1][144:]
        g_in[pl.ds(2048 + 432 * n + 144, 288)] = blocks[2]
        next(big)
    acc = jnp.zeros((3 * CO, 2 * W), F32)
    for f in range(FR):
        rhs = jnp.concatenate([pair(H1, f + 2, 2), jnp.zeros((64, 2 * W), BF16)], axis=0)
        acc = acc + dot_nt(GS[f], rhs)
    for j in range(2):
        g_in[pl.ds(2048 * j + 1728, 288)] = acc[:, j * W:(j + 1) * W].astype(BF16)
    next(big)

    def cot_shift(f, _):
        for r in range(4):
            wide = CE[f, r].astype(F32)
            lanes = pl.ds(r * W, W)
            CS[f, pl.ds(0, CO), lanes] = ahead(wide).astype(BF16)
            CS[f, pl.ds(CO, CO), lanes] = CE[f, r]
            CS[f, pl.ds(2 * CO, CO), lanes] = behind(wide).astype(BF16)
        return 0

    lax.fori_loop(0, 6, cot_shift, 0)

    def cot_window(f, tap):
        kt, kh = TAPS[tap]
        return CS[f + 2 - kt, :, pl.ds((2 - kh) * W, 2 * W)]

    for n in range(2):
        acc = jnp.zeros((CO, 9 * W), F32)
        for f in range(FR):
            rhs = jnp.concatenate([cot_window(f, 4 * n + i) for i in range(4)], axis=0)
            acc = acc + dot_nt(pair(H2, f, 0), rhs)
        for j in range(9):
            g_mid[pl.ds(864 * n + CO * j, CO)] = acc[:, j * W:(j + 1) * W].astype(BF16)
    acc = jnp.zeros((CO, 3 * W), F32)
    for f in range(FR):
        rhs = jnp.concatenate([cot_window(f, 8), jnp.zeros((CO, 2 * W), BF16)], axis=0)
        acc = acc + dot_nt(pair(H2, f, 0), rhs)
    g_mid[pl.ds(1728, CO)] = acc[:, :W].astype(BF16)
    g_mid[pl.ds(1824, CO)] = acc[:, W:2 * W].astype(BF16)
    g_mid[pl.ds(1920, CO)] = (acc[:, 2 * W:] + skip_b).astype(BF16)

    next(small)
    next(big)
    next(small)

    def back_in(f):
        acc = jnp.zeros((3 * CI, 2 * W), F32)
        for n, (kt, kh) in enumerate(TAPS):
            acc = acc + dot(WTI[pl.ds(3 * n, 3)].reshape(3 * CI, CO), pair(GE, f + 2 - kt, 2 - kh))
        skip = lax.dot_general(wskip[...], pair(CE, f, 1), (((0,), (0,)), ((), ())),
                               preferred_element_type=F32)
        for r in range(RW):
            part = acc[:, r * W:(r + 1) * W]
            gh1 = part[CI:2 * CI] + ahead(part[:CI]) + behind(part[2 * CI:])
            grad = norm_pull(XE[2 + f, 1 + r].astype(F32), g1, gh1) + skip[:, r * W:(r + 1) * W]
            OX[f, r] = grad.astype(BF16)

    def turn_in(i, _):
        WTI[i] = WIN[i // 9, (i // 3) % 3, i % 3].astype(F32).T.astype(BF16)
        return 0

    lax.fori_loop(0, 27, turn_in, 0)
    next(big)
    next(small)
    for item in ga_halo:
        item.got()
    for f in range(FR):
        back_in(f)
        if f < 3:
            next(big)
            next(small)
    keep(OX, out_x.at[0])
    for _ in range(3):
        next(big)
        next(small)
    for item in sent:
        item.left()
    for item in kept:
        item.wait()


def assemble(scale, gx_hbm, fi_hbm, fm_hbm, out_x, out_in, out_mid, out_skip, gx, fi, fm, BI, BM, BS, sem, got):
    copies = []

    def put(src, dst):
        copy = pltpu.make_async_copy(src, dst, sem.at[len(copies)])
        copy.start()
        copies.append(copy)

    def load(src, dst, i):
        copy = pltpu.make_async_copy(src, dst, got.at[i])
        copy.start()
        return copy

    need_in = []
    for n in range(5):
        count = 432 if n < 4 else 320
        need_in.append([load(fi_hbm.at[pl.ds(at, count)], fi.at[pl.ds(at, count)], 2 * n + k)
                        for k, at in enumerate((432 * n, 2048 + 432 * n))])
    need_mid = []
    for n in range(5):
        part = pl.ds(480 * n, 480 if n < 4 else 128)
        need_mid.append(load(fm_hbm.at[part], fm.at[part], 10 + n))
    need_x = load(gx_hbm, gx, 15)

    def rows(n, at, count):
        if at + count <= 432:
            value = fi[pl.ds(432 * n + at, count)]
        elif at >= 432:
            value = fi[pl.ds(2048 + 432 * n + at - 432, count)]
        else:
            cut = 432 - at
            value = jnp.concatenate([fi[pl.ds(432 * n + at, cut)], fi[pl.ds(2048 + 432 * n, count - cut)]], axis=0)
        return value.astype(F32) * scale

    for n, taps in enumerate(PAIRS):
        for item in need_in[n]:
            item.wait()
        for kw in range(3):
            low = rows(n, 576 + CO * kw, CO)
            for j, i in enumerate(taps):
                kt, kh = TAPS[i]
                BI[kt, kh, kw, :, pl.ds(0, W)] = rows(n, 288 * j + CO * kw, CO)
                rest = low if j == 0 else pltpu.roll(low, 64, 1)
                BI[kt, kh, kw, :, pl.ds(W, 64)] = rest[:, :64]
        for i in taps:
            put(BI.at[TAPS[i]], out_in.at[TAPS[i]])
    for item in need_in[4]:
        item.wait()
    for kw in range(3):
        BI[2, 2, kw, :, pl.ds(0, W)] = fi[pl.ds(1728 + CO * kw, CO)].astype(F32) * scale
        BI[2, 2, kw, :, pl.ds(W, 64)] = (fi[pl.ds(3776 + CO * kw, CO)].astype(F32) * scale)[:, :64]
    put(BI.at[2, 2], out_in.at[2, 2])
    need_x.wait()
    put(gx, out_x)
    need_mid[4].wait()
    tail = fm[pl.ds(1920, CO)].astype(F32) * scale
    BS[pl.ds(0, 32), pl.ds(0, W)] = fm[pl.ds(2016, 32)].astype(F32) * scale
    BS[pl.ds(32, 32), pl.ds(0, W)] = fi[pl.ds(2016, 32)].astype(F32) * scale
    BS[pl.ds(64, 32), pl.ds(0, W)] = fi[pl.ds(4064, 32)].astype(F32) * scale
    BS[:, pl.ds(W, 64)] = pltpu.roll(tail, 64, 1)[:, :64]
    put(BS, out_skip)
    for j in range(20):
        if j % 5 == 0:
            need_mid[j // 5].wait()
        BM[pl.ds(W * j, W)] = (fm[pl.ds(CO * j, CO)].astype(F32) * scale).T
        if j % 5 == 4:
            rows = pl.ds(W * (j - 4), 5 * W)
            put(BM.at[rows], out_mid.at[rows])
    BM[pl.ds(2560, 32)] = tail.T[:32]
    put(BM.at[pl.ds(2560, 32)], out_mid.at[pl.ds(2560, 32)])
    for copy in copies:
        copy.wait()


def reduce_scratch(rows):
    half = rows // 2
    q, e = half // 8, half // 32
    return {
        "g": (rows, W), "rc": (half, W), "s": (half, W), "a1": (3, q, W), "b1": (3, q, W), "p": (2 * q, W),
        "a2": (3, e, W), "b2": (3, e, W), "c": (2 * e, W), "z": (7, 16, W), "fin": (rows, W),
    }


def shards(inputs, gain_in, conv_in, gain_mid, conv_mid, conv_skip, scored_grads, scored_frames):
    count = scored_frames.shape[1] * inputs.shape[0] * lax.axis_size("dp")
    scale = 1.0 / math.sqrt(count * RW * HT * W)
    anyw = pl.BlockSpec(memory_space=pl.ANY)
    smem = pl.BlockSpec(memory_space=pltpu.SMEM)
    big, small = reduce_scratch(ROWS_IN), reduce_scratch(ROWS_MID)

    def buf(shape, dtype=BF16):
        return pltpu.VMEM(shape, dtype)

    scratch = [
        buf((FR, RW, CI, W)), buf((1, CI), F32), buf((1, CO), F32), buf((CO, CI)),
        buf((6, 4, CI, W)), buf((6, 4, CI, W)), buf((SC * TM, RW, CO, W)), buf((6, 4, CO, W)),
        buf((6, 3 * CO, 4 * W)), buf((6, 4, CO, W)), buf((FR, 3 * CO, RW * W)), buf((2, RW, 3 * CO, 2 * W), F32),
        buf((FR, RW, CO, W)), buf((FR, RW, CO, W)),
        buf((3, 3, 3, CO, CI)), buf((3, 3, 3, CO, CO)), buf((27, CI, CO)), buf((27, CO, CO)),
    ]
    for name in ("g", "rc", "s"):
        scratch += [buf(big[name]), buf(small[name])]
    scratch += [buf(big["a1"]), buf(big["b1"]), buf(small["a1"]), buf(small["b1"])]
    scratch += [buf(big["p"]), buf(small["p"])]
    scratch += [buf(big["a2"]), buf(big["b2"]), buf(small["a2"]), buf(small["b2"])]
    for name in ("c", "z", "fin"):
        scratch += [buf(big[name]), buf(small[name])]
    scratch += [
        pltpu.SemaphoreType.DMA((N_SEMS,)), pltpu.SemaphoreType.DMA((N_SEMS,)),
        pltpu.SemaphoreType.DMA((N_LOCAL,)),
    ]

    def body(*refs):
        kernel(scale, *refs)

    grad_x, sum_in, sum_mid = pl.pallas_call(
        body,
        out_shape=(
            jax.ShapeDtypeStruct(inputs.shape, BF16),
            jax.ShapeDtypeStruct((ROWS_IN, W), BF16),
            jax.ShapeDtypeStruct((ROWS_MID, W), BF16),
        ),
        in_specs=[smem] + [anyw] * 7,
        out_specs=(anyw, anyw, anyw),
        scratch_shapes=scratch,
        compiler_params=pltpu.CompilerParams(
            collective_id=0, has_side_effects=True, vmem_limit_bytes=63 * 1024 * 1024
        ),
        name="block_backward",
    )(scored_frames, inputs, gain_in[None, :], conv_in, gain_mid[None, :], conv_mid, conv_skip, scored_grads)

    def last(*refs):
        assemble(scale, *refs)

    grad_inputs, grad_in, grad_mid, grad_skip = pl.pallas_call(
        last,
        out_shape=(
            jax.ShapeDtypeStruct(inputs.shape, BF16),
            jax.ShapeDtypeStruct(conv_in.shape, F32),
            jax.ShapeDtypeStruct((27 * CO, CO), F32),
            jax.ShapeDtypeStruct(conv_skip.shape, F32),
        ),
        in_specs=[anyw, anyw, anyw],
        out_specs=(anyw, anyw, anyw, anyw),
        scratch_shapes=[
            buf(inputs.shape), buf((ROWS_IN, W)), buf((ROWS_MID, W)),
            buf(conv_in.shape, F32), buf((27 * CO, CO), F32), buf(conv_skip.shape, F32),
            pltpu.SemaphoreType.DMA((16,)), pltpu.SemaphoreType.DMA((16,)),
        ],
        compiler_params=pltpu.CompilerParams(vmem_limit_bytes=63 * 1024 * 1024),
        name="assemble",
    )(grad_x, sum_in, sum_mid)
    return grad_inputs, grad_in, grad_mid.reshape(conv_mid.shape), grad_skip


def solution(mesh):
    in_specs = (
        P("dp", "tm", "height", None, None),
        P(),
        P(),
        P(),
        P(),
        P(),
        P("dp", "tm", "height", None, None),
        P("dp", None),
    )
    out_specs = (P("dp", "tm", "height", None, None), P(), P(), P())
    return jax.shard_map(shards, mesh=mesh, in_specs=in_specs, out_specs=out_specs, check_vma=False)
```
